256 devices in a mesh: seq: 32 (over y, z), grp: 8 (over x, core).
Axes of the slice: x: 4, y: 4, z: 8, core: 2. Of those that a mesh axis runs over, the one named last changes fastest.
Arguments:
- activations: bfloat16 [32768, 4096], P(('grp', 'seq')), parts along dimension 0, may hold values from -6 to 6
- input_weight: bfloat16 [16, 256, 256], replicated, may hold values from -0.375 to 0.375
- decay_weight: bfloat16 [16, 256, 256], replicated, may hold values from -0.375 to 0.375
- input_bias: float32 [4096], replicated, may hold values from -4 to 4
- decay_bias: float32 [4096], replicated, may hold values from -4 to 4
- decay_logits: float32 [4096], replicated, may hold values from -16 to -3
- doc_lengths: int32 [48], P('grp'), parts along dimension 0, may hold values from 1 to 2048, 4096 in all
- cotangent: bfloat16 [32768, 4096], P(('grp', 'seq')), parts along dimension 0, may hold values from -6 to 6
Outputs:
- states: bfloat16 [32768, 4096], P(('grp', 'seq')), parts along dimension 0
- input_grads: bfloat16 [32768, 4096], P(('grp', 'seq')), parts along dimension 0
- input_weight_grads: float32 [32768, 256], P(('grp', 'seq')), parts along dimension 0
- decay_weight_grads: float32 [32768, 256], P(('grp', 'seq')), parts along dimension 0
- input_bias_grads: float32 [32768], P(('grp', 'seq')), parts along dimension 0
- decay_bias_grads: float32 [32768], P(('grp', 'seq')), parts along dimension 0
- decay_logits_grads: float32 [32768], P(('grp', 'seq')), parts along dimension 0
The draws below stay inside these ranges and needn't reach their ends.
There are 8 independent parts, one for each index of `grp`. The reference program is written for one: setup_inputs(seed, part) draws one part's arguments, and reference() takes and returns one part's arrays. A program takes and returns all parts, laid end to end along the dimension named above; an argument that names none is the same for every part. Nothing has to cross between parts.
Inputs may be any that keep to these rules, and one draw needn't show every extreme that they name: `doc_lengths`: the lengths sum to 4096.
All inputs are finite; a program needn't handle non-finite values.
Results may differ from the reference program's by a relative error of at most 0.0034.
Values may be sent and summed in bfloat16 or wider, within the bound.
A program may use at most 128 MiB of HBM per device.

```python
import math
import jax
import jax.numpy as jnp
import numpy as np
from jax import lax

D = 4096
BW = 256
HEADS = 16
SEQ = 4096
DOCS = 6


def draw_decay_logits(key, part):
    key = jax.random.fold_in(key, 11)
    slow_key = jax.random.fold_in(key, 1)
    values = jax.random.uniform(slow_key, (D,), jnp.float32, -16.0, -3.0)
    return values


def with_spikes(entries, key, source, target, parts, factor):
    owner, partner = [(jnp.arange(entries.shape[axis_at]) // (entries.shape[axis_at] // parts)).reshape([-1 if axis == axis_at else 1 for axis in range(entries.ndim)]) for axis_at in (source, target)]
    chosen = jax.random.permutation(key, parts)[partner]
    strong = (owner == chosen) | (owner == (partner + parts // 2) % parts)
    return jnp.where(strong, factor * entries, entries)


def block_levels(own_key, shape, cuts, low, high):
    def one(axis_at, shards_of):
        steps = jax.random.uniform(jax.random.fold_in(jax.random.fold_in(own_key, 6), axis_at), (shards_of,), jnp.float32, low / len(cuts), high / len(cuts))
        return jnp.repeat(jnp.exp(steps), shape[axis_at] // shards_of).reshape((-1,) + (1,) * (len(shape) - axis_at - 1))

    loudness = one(*cuts[0])
    for cut in cuts[1:]:
        loudness = loudness * one(*cut)
    return loudness


def profile(amount, total, limit, skew):
    weights = [(1 << 20) // math.isqrt(grade ** skew) + 1 for grade in range(2, amount + 1)]
    rest, counts = total - limit - (amount - 1), [1] * (amount - 1)
    while rest > 0:
        free = [i for i in range(amount - 1) if counts[i] < limit]
        pool, remaining = sum([weights[i] for i in free]), rest
        for i in free:
            more = min(limit - counts[i], max(1, remaining * weights[i] // pool), rest)
            counts[i] = counts[i] + more
            rest = rest - more
    return np.array([limit] + counts)


def ragged_sizes(own_key, number_of, total, bound, slope):
    if number_of == 2:
        one = jax.random.randint(own_key, (), max(1, total - bound), min(bound, total - 1) + 1)
        return jnp.stack([one, total - one])
    tallies = jnp.asarray(profile(number_of, total, bound, slope), jnp.int32)
    pairs = (number_of - 1) // 2
    donor, taker = tallies[1:1 + 2 * pairs:2], tallies[2:2 + 2 * pairs:2]
    slack = jnp.minimum(donor - 1, bound - taker)
    moved = jax.random.randint(jax.random.fold_in(own_key, 1), (pairs,), 0, 1 << 20) % (slack + 1)
    tallies = tallies.at[1:1 + 2 * pairs:2].set(donor - moved).at[2:2 + 2 * pairs:2].set(taker + moved)
    return tallies[jax.random.permutation(jax.random.fold_in(own_key, 2), number_of)]


def gaussian(key, extent, scale, limit, cuts=(), kind=jnp.bfloat16):
    array = scale * jax.random.normal(key, extent, jnp.float32)
    if cuts:
        array = array * block_levels(key, extent, cuts, -0.22, 0.18)
    return jnp.clip(array, -limit, limit).astype(kind)


def bell_draw_with(key, extent, spread, reach, cuts, heavy, held_as=jnp.bfloat16):
    result = spread * jax.random.normal(key, extent, jnp.float32)
    if cuts:
        result = result * block_levels(key, extent, cuts, -0.22, 0.18)
    return jnp.clip(with_spikes(result, jax.random.fold_in(key, 3), *heavy), -reach, reach).astype(held_as)


def setup_inputs(seed: int = 0, part: int = 0) -> dict:
    arg_keys = jax.random.split(jax.random.key(seed), 9)
    part_keys = jax.random.split(jax.random.fold_in(arg_keys[8], part), 9)
    return {
        "activations": bell_draw_with(part_keys[0], (SEQ, D), 1.0, 6.0, ((0, 32),), (0, 1, 32, 2.75)),
        "input_weight": gaussian(arg_keys[1], (HEADS, BW, BW), BW ** -0.5, 0.375),
        "decay_weight": gaussian(arg_keys[2], (HEADS, BW, BW), BW ** -0.5, 0.375),
        "input_bias": gaussian(arg_keys[3], (D,), 1.0, 4.0, (), jnp.float32),
        "decay_bias": gaussian(arg_keys[4], (D,), 1.0, 4.0, (), jnp.float32),
        "decay_logits": draw_decay_logits(jax.random.fold_in(arg_keys[8], 71), part),
        "doc_lengths": ragged_sizes(part_keys[6], DOCS, SEQ, SEQ // 2, 1).astype(jnp.int32),
        "cotangent": gaussian(part_keys[7], (SEQ, D), 1.0, 6.0, ((0, 32),)),
    }


DECAY_SCALE = 8.0
SQRT_FLOOR = 2.5e-07

def per_block(left, weight):
    rows = left.shape[0]
    heads = weight.shape[0]
    width = weight.shape[1]
    shaped = left.astype(jnp.float32).reshape(rows, heads, width)
    return jnp.einsum('thi,hij->thj', shaped, weight.astype(jnp.float32)).reshape(rows, heads * width)

def per_block_back(grads, weight):
    rows = grads.shape[0]
    heads = weight.shape[0]
    width = weight.shape[1]
    shaped = grads.astype(jnp.float32).reshape(rows, heads, width)
    return jnp.einsum('thj,hij->thi', shaped, weight.astype(jnp.float32)).reshape(rows, heads * width)

def weight_sum(left, grads, heads, width):
    rows = left.shape[0]
    left3 = left.astype(jnp.float32).reshape(rows, heads, width)
    grad3 = grads.astype(jnp.float32).reshape(rows, heads, width)
    return jnp.einsum('thi,thj->hij', left3, grad3).reshape(heads * width, width)

def step_chain(state, pair):
    coef, value = pair
    state = coef * state + value
    return (state, state)

def reference(activations, input_weight, decay_weight, input_bias, decay_bias, decay_logits, doc_lengths, cotangent):
    seq_len = activations.shape[0]
    width_all = activations.shape[1]
    heads = input_weight.shape[0]
    block = input_weight.shape[1]
    starts = (jnp.cumsum(doc_lengths) - doc_lengths).astype(jnp.int32)
    position = jnp.arange(seq_len, dtype=jnp.int32)
    reset = jnp.any(position[:, None] == starts[None, :], axis=1).astype(jnp.float32)[:, None]
    keep = 1.0 - reset
    input_gate = jax.nn.sigmoid(per_block(activations, input_weight) + input_bias)
    decay_gate = jax.nn.sigmoid(per_block(activations, decay_weight) + decay_bias)
    softened = jax.nn.softplus(decay_logits)
    log_decay = -DECAY_SCALE * decay_gate * softened
    decay = jnp.exp(log_decay)
    complement = -jnp.expm1(2.0 * log_decay)
    multiplier = jnp.where(reset > 0.0, 1.0, jnp.sqrt(complement))
    factor = keep * decay
    inputs = activations.astype(jnp.float32)
    pushed = inputs * input_gate * multiplier
    zeros = jnp.zeros((width_all,), jnp.float32)
    _, hidden = lax.scan(step_chain, zeros, (factor, pushed))
    states = hidden.astype(jnp.bfloat16)
    following = jnp.concatenate([factor[1:], jnp.zeros_like(factor[:1])], axis=0)
    _, carried = lax.scan(step_chain, zeros, (following, cotangent.astype(jnp.float32)), reverse=True)
    previous = jnp.concatenate([zeros[None], hidden[:-1]], axis=0)
    dmult = carried * inputs * input_gate
    d_log = keep * (carried * previous * decay - decay * decay * dmult / jnp.sqrt(jnp.maximum(complement, SQRT_FLOOR)))
    pre_input = carried * inputs * multiplier * input_gate * (1.0 - input_gate)
    pre_decay = -DECAY_SCALE * softened * d_log * decay_gate * (1.0 - decay_gate)
    low_input = lax.optimization_barrier(pre_input.astype(jnp.bfloat16))
    low_decay = lax.optimization_barrier(pre_decay.astype(jnp.bfloat16))
    input_grads = carried * input_gate * multiplier + per_block_back(low_input, input_weight) + per_block_back(low_decay, decay_weight)
    input_grads = input_grads.astype(jnp.bfloat16)
    input_weight_grads = weight_sum(activations, low_input, heads, block)
    decay_weight_grads = weight_sum(activations, low_decay, heads, block)
    input_bias_grads = lax.optimization_barrier(jnp.sum(pre_input, axis=0))
    decay_bias_grads = lax.optimization_barrier(jnp.sum(pre_decay, axis=0))
    decay_logits_grads = jax.nn.sigmoid(decay_logits) * lax.optimization_barrier(jnp.sum(-DECAY_SCALE * decay_gate * d_log, axis=0))
    return (states, input_grads, input_weight_grads, decay_weight_grads, input_bias_grads, decay_bias_grads, decay_logits_grads)
```

```python
import jax
import jax.numpy as jnp
from jax import lax
from jax.experimental import pallas as pl
from jax.experimental.pallas import tpu as pltpu
from jax.sharding import PartitionSpec as P

ROWS = 128
WIDTH = 4096
HEADS = 16
BW = 256
DOCS = 6
RING_Y = 4
RING_Z = 8
SEQ_DEVICES = RING_Y * RING_Z
STEPS = 16
GROUPS = 4
ROWS_ZY = 48
ROWS_YZ = ROWS - ROWS_ZY
DECAY_SCALE = 8.0
ROOT_LIMIT = 2000.0
TINY = 1.2e-38
MESH = pl.DeviceIdType.MESH
F32 = jnp.float32
BF16 = jnp.bfloat16

Z_CHAINS = ((0, 1, 4), (0, -1, 3), (1, 1, 3), (1, -1, 4))
Y_CHAINS = ((0, 1, 2), (0, -1, 1), (1, 1, 1), (1, -1, 2))
Z_SUBS = ((4, 3), (-3, 2), (-2, 1), (-1, 0))


def slots_of(chains):
    table, count = {}, 0
    for c, (_, _, hops) in enumerate(chains):
        for i in range(hops):
            table[(c, i)] = count
            count += 1
    return table, count


Z_SLOT, Z_COUNT = slots_of(Z_CHAINS)
Y_SLOT, Y_COUNT = slots_of(Y_CHAINS)


def dot(a, b, dims=((1,), (0,))):
    return lax.dot_general(a, b, (dims, ((), ())), preferred_element_type=F32)


def tile_of(rows):
    pad = jnp.zeros((8 - len(rows), rows[0].shape[1]), F32)
    return jnp.concatenate(list(rows) + [pad], axis=0)


def kernel(
    docs_ref,
    act_hbm,
    wi_hbm,
    wd_hbm,
    bi_ref,
    bd_ref,
    logit_ref,
    cot_hbm,
    states_hbm,
    grads_hbm,
    wgi_ref,
    wgd_ref,
    vec_ref,
    act_v,
    cot_v,
    wi_v,
    wd_v,
    actp,
    cotp,
    fac,
    psh,
    coef,
    quo,
    gin,
    dgate,
    u_s,
    keep_s,
    k8_s,
    perm_s,
    permt_s,
    seg_s,
    states_v,
    grads_v,
    part,
    map_send,
    map_recv,
    rep_send,
    rep_recv,
    bias_send,
    bias_recv,
    z1s,
    z1r,
    y1s,
    y1r,
    z2s,
    z2r,
    y2s,
    y2r,
    in_sem,
    out_sem,
    small_sem,
    z1_ss,
    z1_rs,
    y1_ss,
    y1_rs,
    z2_ss,
    z2_rs,
    y2_ss,
    y2_rs,
):
    me = lax.axis_index("seq")
    y, z = me // RING_Z, lax.rem(me, RING_Z)

    gw = WIDTH // GROUPS
    gh = HEADS // GROUPS
    fetches = []
    for g in range(GROUPS):
        cols = pl.ds(g * gw, gw)
        heads = pl.ds(g * gh, gh)
        pairs = (
            (act_hbm.at[:, cols], act_v.at[:, cols]),
            (wi_hbm.at[heads], wi_v.at[heads]),
            (wd_hbm.at[heads], wd_v.at[heads]),
            (cot_hbm.at[:, cols], cot_v.at[:, cols]),
        )
        group = [
            pltpu.make_async_copy(s, d, in_sem.at[g, i]) for i, (s, d) in enumerate(pairs)
        ]
        for c in group:
            c.start()
        fetches.append(group)

    barrier = pltpu.get_barrier_semaphore()

    def hello(i, carry):
        pl.semaphore_signal(
            barrier,
            inc=1,
            device_id={"seq": lax.rem(me + i, SEQ_DEVICES)},
            device_id_type=MESH,
        )
        return carry

    lax.fori_loop(1, SEQ_DEVICES, hello, 0)

    row = lax.broadcasted_iota(jnp.int32, (ROWS, ROWS), 0)
    col = lax.broadcasted_iota(jnp.int32, (ROWS, ROWS), 1)
    perm_s[...] = (col == (row & 7) * STEPS + (row >> 3)).astype(F32).astype(BF16)
    permt_s[...] = (row == (col & 7) * STEPS + (col >> 3)).astype(F32).astype(BF16)
    seg = lax.broadcasted_iota(jnp.int32, (8, BW), 0)
    first = me * ROWS + seg * STEPS
    starts = [jnp.int32(0)]
    for j in range(DOCS - 1):
        starts.append(starts[-1] + docs_ref[j])
    for k in range(STEPS):
        hit = first + k == starts[0]
        for j in range(1, DOCS):
            hit = hit | (first + k == starts[j])
        keep_s[8 * k : 8 * k + 8, :] = jnp.where(hit, 0.0, 1.0)
    logits = logit_ref[...]
    e = jnp.exp(-jnp.abs(logits))
    series = e * (1.0 + e * (-1 / 2 + e * (1 / 3 + e * (-1 / 4 + e * (1 / 5 + e * (-1 / 6))))))
    soft = jnp.maximum(logits, 0.0) + jnp.where(e < 0.0625, series, jnp.log(1.0 + e))
    k8_s[...] = -DECAY_SCALE * soft

    pl.semaphore_wait(barrier, SEQ_DEVICES - 1)

    def send_tile(src, dst, send_sem, recv_sem, to):
        @pl.when(to != me)
        def _():
            pltpu.make_async_remote_copy(
                src_ref=src.at[to],
                dst_ref=dst.at[me],
                send_sem=send_sem,
                recv_sem=recv_sem,
                device_id={"seq": to},
                device_id_type=MESH,
            ).start()

    def wait_tiles(buf, sem):
        view = buf.at[pl.ds(0, SEQ_DEVICES - 1)]
        pltpu.make_async_copy(view, view, sem).wait()

    def lanes(h):
        return pl.ds(pl.multiple_of(h * BW, BW), BW)

    def phase_a(h, carry):
        sl = lanes(h)
        x = dot(perm_s[...], act_v[:, sl])
        xb = x.astype(BF16)
        actp[h] = xb
        ct = dot(perm_s[...], cot_v[:, sl])
        cotp[h] = ct
        gi = dot(xb, wi_v[h]) + bi_ref[:, sl]
        gd = dot(xb, wd_v[h]) + bd_ref[:, sl]
        k8 = k8_s[:, sl]
        prod = jnp.ones((8, BW), F32)
        fwd = jnp.zeros((8, BW), F32)
        bwd = jnp.zeros((8, BW), F32)
        for k in range(STEPS):
            r = slice(8 * k, 8 * k + 8)
            alive = keep_s[r, :] > 0.0
            xk = x[r]
            ig = 1.0 / (1.0 + jnp.exp(-gi[r]))
            dg = 1.0 / (1.0 + jnp.exp(-gd[r]))
            ld = dg * k8
            dec = jnp.exp(ld)
            t = ld + ld
            near = -t * (1.0 + t * (1 / 2 + t * (1 / 6 + t * (1 / 24))))
            comp = jnp.where(t > -0.0625, near, 1.0 - dec * dec)
            root = lax.rsqrt(jnp.maximum(comp, TINY))
            mult = jnp.where(alive, comp * root, 1.0)
            f = jnp.where(alive, dec, 0.0)
            a = ig * mult
            p = xk * a
            fac[h, r, :] = f
            psh[h, r, :] = p
            coef[h, r, :] = a
            quo[h, r, :] = dec * xk * ig * jnp.minimum(root, ROOT_LIMIT)
            gin[h, r, :] = p * (1.0 - ig)
            dgate[h, r, :] = dg
            fwd = f * fwd + p
            prod = prod * f
            bwd = bwd + prod * ct[r]
        fa, ba = prod, prod
        for d in (1, 2, 4):
            later = seg >= d
            fwd = jnp.where(later, fa * pltpu.roll(fwd, d, 0) + fwd, fwd)
            fa = jnp.where(later, fa * pltpu.roll(fa, d, 0), fa)
            earlier = seg < 8 - d
            bwd = jnp.where(earlier, ba * pltpu.roll(bwd, 8 - d, 0) + bwd, bwd)
            ba = jnp.where(earlier, ba * pltpu.roll(ba, 8 - d, 0), ba)
        whole = tile_of((fa[7:8], fwd[7:8], bwd[0:1]))
        seg_s[h, 0] = jnp.where(seg == 0, 1.0, pltpu.roll(fa, 1, 0))
        seg_s[h, 1] = jnp.where(seg == 0, 0.0, pltpu.roll(fwd, 1, 0))
        seg_s[h, 2] = jnp.where(seg == 7, 1.0, pltpu.roll(ba, 7, 0))
        seg_s[h, 3] = jnp.where(seg == 7, 0.0, pltpu.roll(bwd, 7, 0))
        for half in range(2):
            to = 2 * h + half
            piece = whole[:, half * ROWS : (half + 1) * ROWS]
            map_send[to] = piece

            @pl.when(to == me)
            def _():
                map_recv[me] = piece

            send_tile(map_send, map_recv, small_sem.at[0], small_sem.at[1], to)
        return carry

    for g in range(GROUPS):
        for c in fetches[g]:
            c.wait()
        lax.fori_loop(g * gh, (g + 1) * gh, phase_a, 0)

    wait_tiles(map_recv, small_sem.at[1])
    hid = jnp.zeros((1, ROWS), F32)
    for s in range(SEQ_DEVICES):
        rep_send[s, 0:1, :] = hid
        hid = map_recv[s, 0:1, :] * hid + map_recv[s, 1:2, :]
    back = jnp.zeros((1, ROWS), F32)
    for s in reversed(range(SEQ_DEVICES)):
        rep_send[s, 1:2, :] = back
        back = map_recv[s, 0:1, :] * back + map_recv[s, 2:3, :]
    rep_recv[me] = rep_send[me]

    def reply(i, carry):
        send_tile(
            rep_send, rep_recv, small_sem.at[2], small_sem.at[3], lax.rem(me + i, SEQ_DEVICES)
        )
        return carry

    lax.fori_loop(1, SEQ_DEVICES, reply, 0)
    wait_tiles(rep_recv, small_sem.at[3])

    def phase_b(h, carry):
        sl = lanes(h)
        t0, t1 = rep_recv[2 * h], rep_recv[2 * h + 1]
        hin = jnp.concatenate([t0[0:1], t1[0:1]], axis=1)
        cin = jnp.concatenate([t0[1:2], t1[1:2]], axis=1)
        hid = seg_s[h, 0] * hin + seg_s[h, 1]
        c = seg_s[h, 2] * cin + seg_s[h, 3]
        for k in reversed(range(STEPS)):
            r = slice(8 * k, 8 * k + 8)
            u = cotp[h, r, :] + c
            u_s[r, :] = u
            c = fac[h, r, :] * u
        k8 = k8_s[:, sl]
        sum_i = jnp.zeros((8, BW), F32)
        sum_d = jnp.zeros((8, BW), F32)
        sum_l = jnp.zeros((8, BW), F32)
        hids, lows_i, lows_d, direct = [], [], [], []
        for k in range(STEPS):
            r = slice(8 * k, 8 * k + 8)
            u = u_s[r, :]
            f = fac[h, r, :]
            dg = dgate[h, r, :]
            dl = f * u * (hid - quo[h, r, :]) * dg
            pd = k8 * dl * (1.0 - dg)
            pi = u * gin[h, r, :]
            hid = f * hid + psh[h, r, :]
            sum_i = sum_i + pi
            sum_d = sum_d + pd
            sum_l = sum_l + dl
            hids.append(hid)
            lows_i.append(pi)
            lows_d.append(pd)
            direct.append(u * coef[h, r, :])
        low_i = jnp.concatenate(lows_i, axis=0).astype(BF16)
        low_d = jnp.concatenate(lows_d, axis=0).astype(BF16)
        st = jnp.concatenate(hids, axis=0).astype(BF16)
        states_v[:, sl] = dot(permt_s[...], st).astype(BF16)
        turn = ((1,), (1,))
        ig = jnp.concatenate(direct, axis=0) + dot(low_i, wi_v[h], turn) + dot(low_d, wd_v[h], turn)
        grads_v[:, sl] = dot(permt_s[...], ig.astype(BF16)).astype(BF16)
        both = jnp.concatenate([low_i, low_d], axis=1)
        wg = dot(actp[h], both, ((0,), (0,)))
        part[2 * h] = wg[:ROWS]
        part[2 * h + 1] = wg[ROWS:]
        sums = tile_of(
            [jnp.sum(s, axis=0, keepdims=True) for s in (sum_i, sum_d, sum_l)]
        )
        for half in range(2):
            to = 2 * h + half
            piece = sums[:, half * ROWS : (half + 1) * ROWS]
            bias_send[to] = piece

            @pl.when(to == me)
            def _():
                bias_recv[me] = piece

            send_tile(bias_send, bias_recv, small_sem.at[4], small_sem.at[5], to)
        return carry

    lax.fori_loop(0, HEADS, phase_b, 0)
    stores = [
        pltpu.make_async_copy(states_v, states_hbm, out_sem.at[0]),
        pltpu.make_async_copy(grads_v, grads_hbm, out_sem.at[1]),
    ]
    for c in stores:
        c.start()

    def gcols(g):
        return slice(g * BW, (g + 1) * BW)

    def z_at(off):
        return lax.rem(z + off + RING_Z, RING_Z)

    def y_at(off):
        return lax.rem(y + off + RING_Y, RING_Y)

    sends = []

    def launch(src, dst, ssem, rsem, ty, tz):
        copy = pltpu.make_async_remote_copy(
            src_ref=src,
            dst_ref=dst,
            send_sem=ssem,
            recv_sem=rsem,
            device_id={"seq": ty * RING_Z + tz},
            device_id_type=MESH,
        )
        copy.start()
        sends.append(copy)
        return copy

    z1, y1, z2, y2 = {}, {}, {}, {}

    def z1_send(c, i):
        g, way, hops = Z_CHAINS[c]
        n = Z_SLOT[(c, i)]
        zd = z_at(way * (hops - i))
        if i:
            z1[(c, i - 1)].wait_recv()
        for yd in range(RING_Y):
            v = part[yd * RING_Z + zd, 0:ROWS_ZY, gcols(g)]
            if i:
                v = v + z1r[n - 1, yd].astype(F32)
            z1s[n, yd] = v.astype(BF16)
        z1[(c, i)] = launch(z1s.at[n], z1r.at[n], z1_ss.at[n], z1_rs.at[n], y, z_at(way))

    def z1_fin():
        for c, (g, way, hops) in enumerate(Z_CHAINS):
            z1[(c, hops - 1)].wait_recv()
        for g in range(2):
            ns = [Z_SLOT[(c, ch[2] - 1)] for c, ch in enumerate(Z_CHAINS) if ch[0] == g]
            for yd in range(RING_Y):
                at = yd * RING_Z + z
                part[at, 0:ROWS_ZY, gcols(g)] = part[at, 0:ROWS_ZY, gcols(g)] + (
                    z1r[ns[0], yd].astype(F32) + z1r[ns[1], yd].astype(F32)
                )

    def y1_send(c, i, j):
        g, way, hops = Y_CHAINS[c]
        n = Y_SLOT[(c, i)]
        yd = y_at(way * (hops - i))
        if i:
            y1[(c, i - 1, j)].wait_recv()
        for q, off in enumerate(Z_SUBS[j]):
            v = part[yd * RING_Z + z_at(off), ROWS_ZY:ROWS, gcols(g)]
            if i:
                v = v + y1r[n - 1, j, q].astype(F32)
            y1s[n, j, q] = v.astype(BF16)
        y1[(c, i, j)] = launch(
            y1s.at[n, j], y1r.at[n, j], y1_ss.at[n, j], y1_rs.at[n, j], y_at(way), z
        )

    def y1_init(j):
        for c in (0, 3, 2, 1):
            y1_send(c, 0, j)

    def y1_forward(j):
        for c in (0, 3):
            y1_send(c, 1, j)

    def y1_fin(j):
        for c, (g, way, hops) in enumerate(Y_CHAINS):
            y1[(c, hops - 1, j)].wait_recv()
        for g in range(2):
            ns = [Y_SLOT[(c, ch[2] - 1)] for c, ch in enumerate(Y_CHAINS) if ch[0] == g]
            for q, off in enumerate(Z_SUBS[j]):
                at = y * RING_Z + z_at(off)
                part[at, ROWS_ZY:ROWS, gcols(g)] = part[at, ROWS_ZY:ROWS, gcols(g)] + (
                    y1r[ns[0], j, q].astype(F32) + y1r[ns[1], j, q].astype(F32)
                )

    def z2_step(distance):
        for c, (g, way, hops) in enumerate(Z_CHAINS):
            i = hops - distance
            if i < 0:
                continue
            n = Z_SLOT[(c, i)]
            if i:
                z2[(c, i - 1)].wait_recv()
            v = part[y * RING_Z + z_at(way * distance), ROWS_ZY:ROWS, gcols(g)]
            if i:
                v = v + z2r[n - 1].astype(F32)
            z2s[n] = v.astype(BF16)
            z2[(c, i)] = launch(z2s.at[n], z2r.at[n], z2_ss.at[n], z2_rs.at[n], y, z_at(way))

    def y2_step(distance):
        for c, (g, way, hops) in enumerate(Y_CHAINS):
            i = hops - distance
            if i < 0:
                continue
            n = Y_SLOT[(c, i)]
            if i:
                y2[(c, i - 1)].wait_recv()
            v = part[y_at(way * distance) * RING_Z + z, 0:ROWS_ZY, gcols(g)]
            if i:
                v = v + y2r[n - 1].astype(F32)
            y2s[n] = v.astype(BF16)
            y2[(c, i)] = launch(y2s.at[n], y2r.at[n], y2_ss.at[n], y2_rs.at[n], y_at(way), z)

    y1_init(0)
    for c in range(4):
        z1_send(c, 0)
    y1_init(1)
    y1_forward(0)
    y1_init(2)
    for c in range(4):
        z1_send(c, 1)
    y1_forward(1)
    y1_init(3)
    y1_fin(0)
    z2_step(4)
    for c in range(4):
        z1_send(c, 2)
    y1_forward(2)
    y1_fin(1)
    z2_step(3)
    for c in (0, 3):
        z1_send(c, 3)
    y1_forward(3)
    y1_fin(2)
    z2_step(2)
    z1_fin()
    y2_step(2)
    y2_step(1)
    y1_fin(3)
    z2_step(1)

    wait_tiles(bias_recv, small_sem.at[5])
    total = bias_recv[0]
    for s in range(1, SEQ_DEVICES):
        total = total + bias_recv[s]
    mine = logit_ref[:, pl.ds(pl.multiple_of(me * ROWS, ROWS), ROWS)]
    vec_ref[0:1, :] = total[0:1]
    vec_ref[1:2, :] = total[1:2]
    vec_ref[2:3, :] = total[2:3] * (-DECAY_SCALE / (1.0 + jnp.exp(-mine)))

    outs = (wgi_ref, wgd_ref)
    for c, (g, way, hops) in enumerate(Y_CHAINS):
        y2[(c, hops - 1)].wait_recv()
    for c, (g, way, hops) in enumerate(Z_CHAINS):
        z2[(c, hops - 1)].wait_recv()
    for g in range(2):
        ny = [Y_SLOT[(c, ch[2] - 1)] for c, ch in enumerate(Y_CHAINS) if ch[0] == g]
        nz = [Z_SLOT[(c, ch[2] - 1)] for c, ch in enumerate(Z_CHAINS) if ch[0] == g]
        outs[g][0:ROWS_ZY, :] = part[me, 0:ROWS_ZY, gcols(g)] + (
            y2r[ny[0]].astype(F32) + y2r[ny[1]].astype(F32)
        )
        outs[g][ROWS_ZY:ROWS, :] = part[me, ROWS_ZY:ROWS, gcols(g)] + (
            z2r[nz[0]].astype(F32) + z2r[nz[1]].astype(F32)
        )

    for s in sends:
        s.wait_send()
    wait_tiles(map_send, small_sem.at[0])
    wait_tiles(rep_send, small_sem.at[2])
    wait_tiles(bias_send, small_sem.at[4])
    for c in stores:
        c.wait()


def on_device(act, wi, wd, bi, bd, logits, docs, cot):
    any_spec = pl.BlockSpec(memory_space=pl.ANY)
    vmem = pl.BlockSpec(memory_space=pltpu.VMEM)
    smem = pl.BlockSpec(memory_space=pltpu.SMEM)
    chunk = (HEADS, ROWS, BW)
    scratch = [
        pltpu.VMEM((ROWS, WIDTH), BF16),
        pltpu.VMEM((ROWS, WIDTH), BF16),
        pltpu.VMEM((HEADS, BW, BW), BF16),
        pltpu.VMEM((HEADS, BW, BW), BF16),
        pltpu.VMEM(chunk, BF16),
        pltpu.VMEM(chunk, F32),
        pltpu.VMEM(chunk, F32),
        pltpu.VMEM(chunk, F32),
        pltpu.VMEM(chunk, F32),
        pltpu.VMEM(chunk, F32),
        pltpu.VMEM(chunk, F32),
        pltpu.VMEM(chunk, F32),
        pltpu.VMEM((ROWS, BW), F32),
        pltpu.VMEM((ROWS, BW), F32),
        pltpu.VMEM((1, WIDTH), F32),
        pltpu.VMEM((ROWS, ROWS), BF16),
        pltpu.VMEM((ROWS, ROWS), BF16),
        pltpu.VMEM((HEADS, 4, 8, BW), F32),
        pltpu.VMEM((ROWS, WIDTH), BF16),
        pltpu.VMEM((ROWS, WIDTH), BF16),
        pltpu.VMEM((SEQ_DEVICES, ROWS, 2 * BW), F32),
    ]
    scratch += [pltpu.VMEM((SEQ_DEVICES, 8, ROWS), F32) for _ in range(6)]
    for shape in (
        (Z_COUNT, RING_Y, ROWS_ZY, BW),
        (Y_COUNT, 4, 2, ROWS_YZ, BW),
        (Z_COUNT, ROWS_YZ, BW),
        (Y_COUNT, ROWS_ZY, BW),
    ):
        scratch += [pltpu.VMEM(shape, BF16), pltpu.VMEM(shape, BF16)]
    scratch += [
        pltpu.SemaphoreType.DMA((GROUPS, 4)),
        pltpu.SemaphoreType.DMA((2,)),
        pltpu.SemaphoreType.DMA((6,)),
    ]
    for shape in ((Z_COUNT,), (Y_COUNT, 4), (Z_COUNT,), (Y_COUNT,)):
        scratch += [pltpu.SemaphoreType.DMA(shape), pltpu.SemaphoreType.DMA(shape)]
    states, grads, wgi, wgd, vec = pl.pallas_call(
        kernel,
        out_shape=(
            jax.ShapeDtypeStruct((ROWS, WIDTH), BF16),
            jax.ShapeDtypeStruct((ROWS, WIDTH), BF16),
            jax.ShapeDtypeStruct((ROWS, BW), F32),
            jax.ShapeDtypeStruct((ROWS, BW), F32),
            jax.ShapeDtypeStruct((8, ROWS), F32),
        ),
        in_specs=[smem, any_spec, any_spec, any_spec, vmem, vmem, vmem, any_spec],
        out_specs=(any_spec, any_spec, vmem, vmem, vmem),
        scratch_shapes=scratch,
        compiler_params=pltpu.CompilerParams(
            collective_id=0, has_side_effects=True, vmem_limit_bytes=60 * 1024 * 1024
        ),
    )(
        docs,
        act,
        wi,
        wd,
        bi.reshape(1, WIDTH),
        bd.reshape(1, WIDTH),
        logits.reshape(1, WIDTH),
        cot,
    )
    return states, grads, wgi, wgd, vec[0], vec[1], vec[2]


def solution(mesh):
    rows = P(("grp", "seq"), None)
    flat = P(("grp", "seq"))
    return jax.shard_map(
        on_device,
        mesh=mesh,
        in_specs=(rows, P(), P(), P(), P(), P(), P("grp"), rows),
        out_specs=(rows, rows, rows, rows, flat, flat, flat),
        check_vma=False,
    )
```

```python
import jax
import jax.numpy as jnp
from jax import lax
from jax.experimental import pallas as pl
from jax.experimental.pallas import tpu as pltpu
from jax.sharding import PartitionSpec as P

ROWS = 128
WIDTH = 4096
HEADS = 16
BW = 256
DOCS = 6
RING_Y = 4
RING_Z = 8
SEQ_DEVICES = RING_Y * RING_Z
STEPS = 16
GROUPS = 4
ZY = 128
YZ = 2 * BW - ZY
HALF = ROWS // 2
DECAY_SCALE = 8.0
ROOT_LIMIT = 2000.0
TINY = 1.2e-38
MESH = pl.DeviceIdType.MESH
F32 = jnp.float32
BF16 = jnp.bfloat16

Z_CHAINS = ((0, 1, 4), (0, -1, 3), (1, 1, 3), (1, -1, 4))
LOG2E = 1.4426950408889634
LN2 = 0.6931471805599453
RESET = -1e4


def slots_of(chains):
    table, count = {}, 0
    for c, (_, _, hops) in enumerate(chains):
        for i in range(hops):
            table[(c, i)] = count
            count += 1
    return table, count


Z_SLOT, Z_COUNT = slots_of(Z_CHAINS)


def dot(a, b, dims=((1,), (0,))):
    return lax.dot_general(a, b, (dims, ((), ())), preferred_element_type=F32)


def recip(x):
    return pltpu.reciprocal(x, approx=True)


def tile_of(rows):
    pad = jnp.zeros((8 - len(rows), rows[0].shape[1]), F32)
    return jnp.concatenate(list(rows) + [pad], axis=0)


def kernel(
    docs_ref,
    act_hbm,
    wi_hbm,
    wd_hbm,
    bi_ref,
    bd_ref,
    logit_ref,
    cot_hbm,
    states_hbm,
    grads_hbm,
    wgi_ref,
    wgd_ref,
    vec_ref,
    act_v,
    cot_v,
    w_v,
    actp,
    cotp,
    fac,
    psh,
    coef,
    quo,
    gin,
    dgate,
    low_s,
    st_s,
    u_s,
    reset_s,
    k8_s,
    perm_s,
    permt_s,
    seg_s,
    states_v,
    grads_v,
    part,
    prods,
    pair_a,
    pair_b,
    gates_a,
    gates_b,
    act_all,
    low_all,
    map_send,
    map_recv,
    rep_send,
    rep_recv,
    bias_send,
    bias_recv,
    z1s,
    z1r,
    z2s,
    z2r,
    y2s,
    y2r,
    in_sem,
    out_sem,
    small_sem,
    z1_ss,
    z1_rs,
    z2_ss,
    z2_rs,
    y2_ss,
    y2_rs,
    act_ss,
    act_rs,
    low_ss,
    low_rs,
):
    me = lax.axis_index("seq")
    y, z = me // RING_Z, lax.rem(me, RING_Z)

    gw = WIDTH // GROUPS
    gh = HEADS // GROUPS

    def fetch(g):
        cols = pl.ds(pl.multiple_of(g * gw, gw), gw)
        heads = pl.ds(g * gh, gh)
        pairs = (
            (act_hbm.at[:, cols], act_v.at[:, cols]),
            (wi_hbm.at[heads], w_v.at[heads, :, 0:BW]),
            (wd_hbm.at[heads], w_v.at[heads, :, BW:]),
            (cot_hbm.at[:, cols], cot_v.at[:, cols]),
        )
        return [pltpu.make_async_copy(s, d, in_sem.at[g, i]) for i, (s, d) in enumerate(pairs)]

    for g in range(GROUPS):
        for c in fetch(g):
            c.start()

    barrier = pltpu.get_barrier_semaphore()

    def hello(i, carry):
        pl.semaphore_signal(
            barrier,
            inc=1,
            device_id={"seq": lax.rem(me + i, SEQ_DEVICES)},
            device_id_type=MESH,
        )
        return carry

    lax.fori_loop(1, SEQ_DEVICES, hello, 0)

    row = lax.broadcasted_iota(jnp.int32, (ROWS, ROWS), 0)
    col = lax.broadcasted_iota(jnp.int32, (ROWS, ROWS), 1)
    perm_s[...] = (col == (row & 7) * STEPS + (row >> 3)).astype(F32).astype(BF16)
    permt_s[...] = (row == (col & 7) * STEPS + (col >> 3)).astype(F32).astype(BF16)
    seg = lax.broadcasted_iota(jnp.int32, (8, BW), 0)
    first = me * ROWS + seg * STEPS
    starts = [jnp.int32(0)]
    for j in range(DOCS - 1):
        starts.append(starts[-1] + docs_ref[j])
    for k in range(STEPS):
        hit = first + k == starts[0]
        for j in range(1, DOCS):
            hit = hit | (first + k == starts[j])
        reset_s[8 * k : 8 * k + 8, :] = jnp.where(hit, RESET, 0.0)
    logits = logit_ref[...]
    e = jnp.exp(-jnp.abs(logits))
    series = e * (1.0 + e * (-1 / 2 + e * (1 / 3 + e * (-1 / 4 + e * (1 / 5 + e * (-1 / 6))))))
    soft = jnp.maximum(logits, 0.0) + jnp.where(e < 0.0625, series, jnp.log(1.0 + e))
    k8_s[...] = -DECAY_SCALE * soft

    def send_tile(src, dst, send_sem, recv_sem, to):
        @pl.when(to != me)
        def _():
            pltpu.make_async_remote_copy(
                src_ref=src.at[to],
                dst_ref=dst.at[me],
                send_sem=send_sem,
                recv_sem=recv_sem,
                device_id={"seq": to},
                device_id_type=MESH,
            ).start()

    def wait_tiles(buf, sem, n=8):
        view = buf.at[pl.ds(0, SEQ_DEVICES - 1), 0:n]
        pltpu.make_async_copy(view, view, sem).wait()

    def lanes(h):
        return pl.ds(pl.multiple_of(h * BW, BW), BW)

    def gate_dots(h, pair_s, gates_s):
        sl = lanes(h)

        @pl.when(lax.rem(h, gh) == 0)
        def _():
            for c in fetch(h // gh):
                c.wait()

        pair = dot(perm_s[...], jnp.concatenate([act_v[:, sl], cot_v[:, sl]], axis=1))
        pair_s[...] = pair
        xb = pair[:, :BW].astype(BF16)
        actp[h] = xb
        gates_s[...] = dot(xb, w_v[h])

    def local_maps(h, pair_s, gates_s):
        sl = lanes(h)
        bi, bd = bi_ref[:, sl], bd_ref[:, sl]
        k8 = k8_s[:, sl] * LOG2E
        prod = jnp.ones((8, BW), F32)
        fwd = jnp.zeros((8, BW), F32)
        bwd = jnp.zeros((8, BW), F32)
        for k in range(STEPS):
            r = slice(8 * k, 8 * k + 8)
            xk = pair_s[r, :BW]
            ct = pair_s[r, BW:]
            cotp[h, r, :] = ct
            ig = recip(1.0 + jnp.exp2((gates_s[r, :BW] + bi) * -LOG2E))
            dg = recip(1.0 + jnp.exp2((gates_s[r, BW:] + bd) * -LOG2E))
            ld = dg * k8 + reset_s[r, :]
            f = jnp.exp2(ld)
            th = jnp.tanh(ld * -LN2)
            comp = th + th * (f * f)
            root = lax.rsqrt(jnp.maximum(comp, TINY))
            a = ig * (comp * root)
            p = xk * a
            fac[h, r, :] = f
            psh[h, r, :] = p
            coef[h, r, :] = a
            quo[h, r, :] = f * (xk * ig) * jnp.minimum(root, ROOT_LIMIT)
            gin[h, r, :] = p * (1.0 - ig)
            dgate[h, r, :] = dg
            fwd = f * fwd + p
            prod = prod * f
            bwd = bwd + prod * ct
        fa, ba = prod, prod
        for d in (1, 2, 4):
            later = seg >= d
            fwd = jnp.where(later, fa * pltpu.roll(fwd, d, 0) + fwd, fwd)
            fa = jnp.where(later, fa * pltpu.roll(fa, d, 0), fa)
            earlier = seg < 8 - d
            bwd = jnp.where(earlier, ba * pltpu.roll(bwd, 8 - d, 0) + bwd, bwd)
            ba = jnp.where(earlier, ba * pltpu.roll(ba, 8 - d, 0), ba)
        whole = tile_of((fa[7:8], fwd[7:8], bwd[0:1]))
        seg_s[h, 0] = jnp.where(seg == 0, 1.0, pltpu.roll(fa, 1, 0))
        seg_s[h, 1] = jnp.where(seg == 0, 0.0, pltpu.roll(fwd, 1, 0))
        seg_s[h, 2] = jnp.where(seg == 7, 1.0, pltpu.roll(ba, 7, 0))
        seg_s[h, 3] = jnp.where(seg == 7, 0.0, pltpu.roll(bwd, 7, 0))
        for half in range(2):
            map_send[2 * h + half] = whole[:, half * ROWS : (half + 1) * ROWS]

    def share(h):
        for half in range(2):
            to = 2 * h + half

            @pl.when(to == me)
            def _():
                map_recv[me] = map_send[me]

            send_tile(map_send, map_recv, small_sem.at[0], small_sem.at[1], to)
        yd, q = h // (RING_Z // 2), lax.rem(h, RING_Z // 2)
        d = lax.rem(yd - y + RING_Y, RING_Y)

        @pl.when(d == 0)
        def _():
            act_all[q, 0] = actp[h]

        @pl.when(d != 0)
        def _():
            pltpu.make_async_remote_copy(
                src_ref=actp.at[h],
                dst_ref=act_all.at[q, d],
                send_sem=act_ss.at[q, d],
                recv_sem=act_rs.at[q, d],
                device_id={"seq": yd * RING_Z + z},
                device_id_type=MESH,
            ).start()

    def two_heads(i, carry):
        gate_dots(2 * i + 1, pair_b, gates_b)
        local_maps(2 * i, pair_a, gates_a)
        gate_dots(2 * i + 2 - (2 * i + 2) // HEADS, pair_a, gates_a)
        local_maps(2 * i + 1, pair_b, gates_b)
        return carry

    def two_heads_and_share(i, carry):
        two_heads(i, carry)
        for k in range(2):
            share(2 * i + k - HEADS // 2)
            share(2 * i + k)
        return carry

    gate_dots(0, pair_a, gates_a)
    lax.fori_loop(0, HEADS // 4, two_heads, 0)
    pl.semaphore_wait(barrier, SEQ_DEVICES - 1)
    lax.fori_loop(HEADS // 4, HEADS // 2, two_heads_and_share, 0)

    wait_tiles(map_recv, small_sem.at[1])
    hid = jnp.zeros((1, ROWS), F32)
    for s in range(SEQ_DEVICES):
        rep_send[s, 0:1, :] = hid
        hid = map_recv[s, 0:1, :] * hid + map_recv[s, 1:2, :]
    back = jnp.zeros((1, ROWS), F32)
    for s in reversed(range(SEQ_DEVICES)):
        rep_send[s, 1:2, :] = back
        back = map_recv[s, 0:1, :] * back + map_recv[s, 2:3, :]
    rep_recv[me, 0:2] = rep_send[me, 0:2]

    def reply(i, carry):
        to = lax.rem(me + i, SEQ_DEVICES)
        pltpu.make_async_remote_copy(
            src_ref=rep_send.at[to, 0:2],
            dst_ref=rep_recv.at[me, 0:2],
            send_sem=small_sem.at[2],
            recv_sem=small_sem.at[3],
            device_id={"seq": to},
            device_id_type=MESH,
        ).start()
        return carry

    lax.fori_loop(1, SEQ_DEVICES, reply, 0)
    wait_tiles(rep_recv, small_sem.at[3], 2)

    def chains(h):
        sl = lanes(h)
        t0, t1 = rep_recv[2 * h], rep_recv[2 * h + 1]
        hin = jnp.concatenate([t0[0:1], t1[0:1]], axis=1)
        cin = jnp.concatenate([t0[1:2], t1[1:2]], axis=1)
        hid = seg_s[h, 0] * hin + seg_s[h, 1]
        c = seg_s[h, 2] * cin + seg_s[h, 3]
        for k in reversed(range(STEPS)):
            r = slice(8 * k, 8 * k + 8)
            u = cotp[h, r, :] + c
            u_s[r, :] = u
            c = fac[h, r, :] * u
        k8 = k8_s[:, sl]
        sum_i = jnp.zeros((8, BW), F32)
        sum_d = jnp.zeros((8, BW), F32)
        sum_l = jnp.zeros((8, BW), F32)
        hids, lows_i, lows_d = [], [], []
        for k in range(STEPS):
            r = slice(8 * k, 8 * k + 8)
            u = u_s[r, :]
            f = fac[h, r, :]
            dg = dgate[h, r, :]
            dl = f * u * (hid - quo[h, r, :]) * dg
            pd = k8 * dl * (1.0 - dg)
            pi = u * gin[h, r, :]
            hid = f * hid + psh[h, r, :]
            sum_i = sum_i + pi
            sum_d = sum_d + pd
            sum_l = sum_l + dl
            hids.append(hid)
            lows_i.append(pi)
            lows_d.append(pd)
            coef[h, r, :] = u * coef[h, r, :]
        low_i = jnp.concatenate(lows_i, axis=0).astype(BF16)
        low_d = jnp.concatenate(lows_d, axis=0).astype(BF16)
        st_s[h] = jnp.concatenate(hids, axis=0).astype(BF16)
        both = jnp.concatenate([low_i, low_d], axis=1)
        low_s[h] = both
        wg = dot(actp[h], both[:, YZ:], ((0,), (0,)))
        part[2 * h] = wg[:ROWS]
        part[2 * h + 1] = wg[ROWS:]
        sums = tile_of(
            [jnp.sum(s, axis=0, keepdims=True) for s in (sum_i, sum_d, sum_l)]
        )
        for half in range(2):
            to = 2 * h + half
            piece = sums[:, half * ROWS : (half + 1) * ROWS]
            bias_send[to] = piece

            @pl.when(to == me)
            def _():
                bias_recv[me] = piece

            send_tile(bias_send, bias_recv, small_sem.at[4], small_sem.at[5], to)

    zp, odd = z // 2, lax.rem(z, 2)

    def group_of(j):
        return lax.rem(zp + (2, 1 + 2 * odd, 3 - 2 * odd, 0)[j], RING_Z // 2)

    def make_group(j):
        q = group_of(j)

        def one(i, carry):
            d = lax.rem(i + 2, RING_Y)
            yd = lax.rem(y + d, RING_Y)
            h = yd * (RING_Z // 2) + q
            chains(h)

            @pl.when(d == 0)
            def _():
                low_all[q, 0] = low_s[h, :, :YZ]

            @pl.when(d != 0)
            def _():
                pltpu.make_async_remote_copy(
                    src_ref=low_s.at[h, :, pl.ds(0, YZ)],
                    dst_ref=low_all.at[q, d],
                    send_sem=low_ss.at[j, d],
                    recv_sem=low_rs.at[j, d],
                    device_id={"seq": yd * RING_Z + z},
                    device_id_type=MESH,
                ).start()

            return carry

        lax.fori_loop(0, RING_Y, one, 0)

    def finish(h, carry):
        sl = lanes(h)
        ig = coef[h] + dot(low_s[h], w_v[h], ((1,), (1,)))
        out = dot(permt_s[...], jnp.concatenate([st_s[h], ig.astype(BF16)], axis=1)).astype(BF16)
        states_v[:, sl] = out[:, :BW]
        grads_v[:, sl] = out[:, BW:]
        return carry

    def finish_quarter(i):
        lax.fori_loop(i * HEADS // 4, (i + 1) * HEADS // 4, finish, 0)

    def half(p):
        return slice(p * HALF, (p + 1) * HALF)

    def landed(buf, sem):
        pltpu.make_async_copy(buf, buf, sem).wait()

    def z_at(off):
        return lax.rem(z + off + RING_Z, RING_Z)

    def y_at(off):
        return lax.rem(y + off + RING_Y, RING_Y)

    sends = []

    def launch(src, dst, ssem, rsem, ty, tz):
        copy = pltpu.make_async_remote_copy(
            src_ref=src,
            dst_ref=dst,
            send_sem=ssem,
            recv_sem=rsem,
            device_id={"seq": ty * RING_Z + tz},
            device_id_type=MESH,
        )
        copy.start()
        sends.append(copy)
        return copy

    z1, z2, y2 = {}, {}, {}

    def z1_send(c, i):
        p, way, hops = Z_CHAINS[c]
        n = Z_SLOT[(c, i)]
        zd = z_at(way * (hops - i))
        if i:
            z1[(c, i - 1)].wait_recv()
        for d in range(RING_Y):
            v = part[y_at(d) * RING_Z + zd, half(p), :]
            if i:
                v = v + z1r[n - 1, d].astype(F32)
            z1s[n, d] = v.astype(BF16)
        z1[(c, i)] = launch(z1s.at[n], z1r.at[n], z1_ss.at[n], z1_rs.at[n], y, z_at(way))

    def last_of(p):
        return [Z_SLOT[(c, ch[2] - 1)] for c, ch in enumerate(Z_CHAINS) if ch[0] == p]

    def z1_fin():
        for c, (p, way, hops) in enumerate(Z_CHAINS):
            z1[(c, hops - 1)].wait_recv()
        for p in range(2):
            n, m = last_of(p)
            for d in range(RING_Y):
                v = part[y_at(d) * RING_Z + z, half(p), :] + (
                    z1r[n, d].astype(F32) + z1r[m, d].astype(F32)
                )
                if d:
                    y2s[d, half(p), :] = v.astype(BF16)
                else:
                    part[me, half(p), :] = v
        for d in (2, 1, 3):
            y2[d] = launch(y2s.at[d], y2r.at[d], y2_ss.at[d], y2_rs.at[d], y_at(d), z)

    def product(j):
        q = group_of(j)
        for d in range(1, RING_Y):
            if j == 0:
                for k in range(RING_Z // 2):
                    landed(act_all.at[k, d], act_rs.at[k, d])
            landed(low_all.at[q, d], low_rs.at[j, d])
        acts = act_all[q].reshape(RING_Y * ROWS, BW)
        lows = low_all[q].reshape(RING_Y * ROWS, YZ)
        wg = dot(acts, lows, ((0,), (0,)))
        prods[2 * q] = wg[:ROWS]
        prods[2 * q + 1] = wg[ROWS:]

    def z2_step(distance):
        for c, (p, way, hops) in enumerate(Z_CHAINS):
            i = hops - distance
            if i < 0:
                continue
            n = Z_SLOT[(c, i)]
            if i:
                z2[(c, i - 1)].wait_recv()
            v = prods[z_at(way * distance), half(p), :]
            if i:
                v = v + z2r[n - 1].astype(F32)
            z2s[n] = v.astype(BF16)
            z2[(c, i)] = launch(z2s.at[n], z2r.at[n], z2_ss.at[n], z2_rs.at[n], y, z_at(way))

    def z1_sends(*which):
        for c, i in which:
            z1_send(c, i)

    make_group(0)
    z1_sends((0, 0), (3, 0))
    make_group(1)
    z1_sends((1, 0), (2, 0))
    make_group(2)
    z1_sends((0, 1), (3, 1))
    make_group(3)
    z1_sends((1, 1), (2, 1))
    product(0)
    z2_step(4)
    z1_sends((0, 2), (3, 2))
    finish_quarter(0)
    z1_sends((1, 2), (2, 2), (0, 3), (3, 3))
    product(1)
    z2_step(3)
    finish_quarter(1)
    z1_fin()
    finish_quarter(2)
    product(2)
    z2_step(2)
    finish_quarter(3)
    stores = [
        pltpu.make_async_copy(states_v, states_hbm, out_sem.at[0]),
        pltpu.make_async_copy(grads_v, grads_hbm, out_sem.at[1]),
    ]
    for c in stores:
        c.start()
    product(3)
    z2_step(1)

    wait_tiles(bias_recv, small_sem.at[5])
    total = bias_recv[0]
    for s in range(1, SEQ_DEVICES):
        total = total + bias_recv[s]
    mine = logit_ref[:, pl.ds(pl.multiple_of(me * ROWS, ROWS), ROWS)]
    vec_ref[0:1, :] = total[0:1]
    vec_ref[1:2, :] = total[1:2]
    vec_ref[2:3, :] = total[2:3] * (-DECAY_SCALE / (1.0 + jnp.exp(-mine)))

    for d in range(1, RING_Y):
        y2[d].wait_recv()
    rest = part[me] + (y2r[1].astype(F32) + y2r[2].astype(F32) + y2r[3].astype(F32))
    wgd_ref[:, 2 * BW - YZ :] = rest
    for c, (p, way, hops) in enumerate(Z_CHAINS):
        z2[(c, hops - 1)].wait_recv()
    for p in range(2):
        n, m = last_of(p)
        done = prods[z, half(p), :] + (z2r[n].astype(F32) + z2r[m].astype(F32))
        wgi_ref[half(p), :] = done[:, :BW]
        wgd_ref[half(p), : YZ - BW] = done[:, BW:]

    for s in sends:
        s.wait_send()
    for d in range(1, RING_Y):
        for k in range(RING_Z // 2):
            landed(act_all.at[k, d], act_ss.at[k, d])
            landed(low_all.at[k, d], low_ss.at[k, d])
    wait_tiles(map_send, small_sem.at[0])
    wait_tiles(rep_send, small_sem.at[2], 2)
    wait_tiles(bias_send, small_sem.at[4])
    for c in stores:
        c.wait()


def hand_over(*refs):
    ins, outs, sem = refs[:5], refs[5:12], refs[12]
    pairs = list(zip(ins[:4], outs[:4]))
    pairs += [(ins[4].at[pl.ds(i, 1)], outs[4 + i]) for i in range(3)]
    copies = [pltpu.make_async_copy(s, d, sem.at[i]) for i, (s, d) in enumerate(pairs)]
    for c in copies:
        c.start()
    for c in copies:
        c.wait()


def on_device(act, wi, wd, bi, bd, logits, docs, cot):
    any_spec = pl.BlockSpec(memory_space=pl.ANY)
    vmem = pl.BlockSpec(memory_space=pltpu.VMEM)
    smem = pl.BlockSpec(memory_space=pltpu.SMEM)
    chunk = (HEADS, ROWS, BW)
    scratch = [
        pltpu.VMEM((ROWS, WIDTH), BF16),
        pltpu.VMEM((ROWS, WIDTH), BF16),
        pltpu.VMEM((HEADS, BW, 2 * BW), BF16),
        pltpu.VMEM(chunk, BF16),
        pltpu.VMEM(chunk, F32),
        pltpu.VMEM(chunk, F32),
        pltpu.VMEM(chunk, F32),
        pltpu.VMEM(chunk, F32),
        pltpu.VMEM(chunk, F32),
        pltpu.VMEM(chunk, F32),
        pltpu.VMEM(chunk, F32),
        pltpu.VMEM((HEADS, ROWS, 2 * BW), BF16),
        pltpu.VMEM(chunk, BF16),
        pltpu.VMEM((ROWS, BW), F32),
        pltpu.VMEM((ROWS, BW), F32),
        pltpu.VMEM((1, WIDTH), F32),
        pltpu.VMEM((ROWS, ROWS), BF16),
        pltpu.VMEM((ROWS, ROWS), BF16),
        pltpu.VMEM((HEADS, 4, 8, BW), F32),
        pltpu.VMEM((ROWS, WIDTH), BF16),
        pltpu.VMEM((ROWS, WIDTH), BF16),
        pltpu.VMEM((SEQ_DEVICES, ROWS, ZY), F32),
        pltpu.VMEM((RING_Z, ROWS, YZ), F32),
        pltpu.VMEM((ROWS, 2 * BW), F32),
        pltpu.VMEM((ROWS, 2 * BW), F32),
        pltpu.VMEM((ROWS, 2 * BW), F32),
        pltpu.VMEM((ROWS, 2 * BW), F32),
        pltpu.VMEM((RING_Z // 2, RING_Y, ROWS, BW), BF16),
        pltpu.VMEM((RING_Z // 2, RING_Y, ROWS, YZ), BF16),
    ]
    scratch += [pltpu.VMEM((SEQ_DEVICES, 8, ROWS), F32) for _ in range(6)]
    for shape in (
        (Z_COUNT, RING_Y, HALF, ZY),
        (Z_COUNT, HALF, YZ),
        (RING_Y, ROWS, ZY),
    ):
        scratch += [pltpu.VMEM(shape, BF16), pltpu.VMEM(shape, BF16)]
    scratch += [
        pltpu.SemaphoreType.DMA((GROUPS, 4)),
        pltpu.SemaphoreType.DMA((2,)),
        pltpu.SemaphoreType.DMA((6,)),
    ]
    quads = (RING_Z // 2, RING_Y)
    for shape in ((Z_COUNT,), (Z_COUNT,), (RING_Y,), quads, quads):
        scratch += [pltpu.SemaphoreType.DMA(shape), pltpu.SemaphoreType.DMA(shape)]
    states, grads, wgi, wgd, vec = pl.pallas_call(
        kernel,
        out_shape=(
            jax.ShapeDtypeStruct((ROWS, WIDTH), BF16),
            jax.ShapeDtypeStruct((ROWS, WIDTH), BF16),
            jax.ShapeDtypeStruct((ROWS, BW), F32),
            jax.ShapeDtypeStruct((ROWS, BW), F32),
            jax.ShapeDtypeStruct((8, ROWS), F32),
        ),
        in_specs=[smem, any_spec, any_spec, any_spec, vmem, vmem, vmem, any_spec],
        out_specs=(any_spec, any_spec, vmem, vmem, vmem),
        scratch_shapes=scratch,
        compiler_params=pltpu.CompilerParams(
            collective_id=0, has_side_effects=True, vmem_limit_bytes=60 * 1024 * 1024
        ),
    )(
        docs,
        act,
        wi,
        wd,
        bi.reshape(1, WIDTH),
        bd.reshape(1, WIDTH),
        logits.reshape(1, WIDTH),
        cot,
    )
    outs = pl.pallas_call(
        hand_over,
        out_shape=[jax.ShapeDtypeStruct(a.shape, a.dtype) for a in (states, grads, wgi, wgd)]
        + [jax.ShapeDtypeStruct((1, ROWS), F32)] * 3,
        in_specs=[vmem] * 5,
        out_specs=[any_spec] * 7,
        scratch_shapes=[pltpu.SemaphoreType.DMA((7,))],
    )(states, grads, wgi, wgd, vec)
    return (*outs[:4], *(v.reshape(ROWS) for v in outs[4:]))


def solution(mesh):
    rows = P(("grp", "seq"), None)
    flat = P(("grp", "seq"))
    return jax.shard_map(
        on_device,
        mesh=mesh,
        in_specs=(rows, P(), P(), P(), P(), P(), P("grp"), rows),
        out_specs=(rows, rows, rows, rows, flat, flat, flat),
        check_vma=False,
    )
```

```python
import functools

import jax
import jax.numpy as jnp
from jax import lax
from jax.experimental import pallas as pl
from jax.experimental.pallas import tpu as pltpu
from jax.sharding import PartitionSpec as P

ROWS = 128
WIDTH = 4096
HEADS = 16
BW = 256
DOCS = 6
RING_Y = 4
RING_Z = 8
SEQ_DEVICES = RING_Y * RING_Z
STEPS = 16
GROUPS = 4
ZY = 128
YZ = 2 * BW - ZY
HALF = ROWS // 2
DECAY_SCALE = 8.0
ROOT_LIMIT = 2000.0
TINY = 1.2e-38
MESH = pl.DeviceIdType.MESH
F32 = jnp.float32
BF16 = jnp.bfloat16

Z_CHAINS = ((0, 1, 4), (0, -1, 3), (1, 1, 3), (1, -1, 4))
LOG2E = 1.4426950408889634
LN2 = 0.6931471805599453
RESET = -1e4
ACT_EARLY = ((2, 0), (2, 1))
ACT_LATE = ((1, 0), (3, 0), (1, 1), (3, 1))


def slots_of(chains):
    table, count = {}, 0
    for c, (_, _, hops) in enumerate(chains):
        for i in range(hops):
            table[(c, i)] = count
            count += 1
    return table, count


Z_SLOT, Z_COUNT = slots_of(Z_CHAINS)


def dot(a, b, dims=((1,), (0,))):
    return lax.dot_general(a, b, (dims, ((), ())), preferred_element_type=F32)


def recip(x):
    return pltpu.reciprocal(x, approx=True)


def tile_of(rows):
    pad = jnp.zeros((8 - len(rows), rows[0].shape[1]), F32)
    return jnp.concatenate(list(rows) + [pad], axis=0)


def kernel(
    docs_ref,
    act_hbm,
    wi_hbm,
    wd_hbm,
    bi_ref,
    bd_ref,
    logit_ref,
    cot_hbm,
    states_v,
    grads_v,
    wgi_ref,
    wgd_ref,
    vec_ref,
    act_v,
    cot_v,
    w_v,
    cotp,
    fac,
    psh,
    coef,
    quo,
    gin,
    dgate,
    direct,
    low_s,
    u_s,
    stage,
    reset_s,
    k8_s,
    seg_s,
    part,
    prods,
    in_a,
    in_b,
    act_all,
    low_all,
    map_send,
    map_recv,
    rep_send,
    rep_recv,
    bias_send,
    bias_recv,
    z1s,
    z1r,
    z2s,
    z2r,
    y2s,
    y2r,
    in_sem,
    small_sem,
    z1_ss,
    z1_rs,
    z2_ss,
    z2_rs,
    y2_ss,
    y2_rs,
    act_ss,
    act_rs,
    low_ss,
    low_rs,
    rep_rs,
):
    me = lax.axis_index("seq")
    y, z = me // RING_Z, lax.rem(me, RING_Z)

    gw = WIDTH // GROUPS
    gh = HEADS // GROUPS

    def fetch(g):
        cols = pl.ds(pl.multiple_of(g * gw, gw), gw)
        heads = pl.ds(g * gh, gh)
        pairs = (
            (act_hbm.at[:, cols], act_v.at[:, cols]),
            (wi_hbm.at[heads], w_v.at[heads, :, 0:BW]),
            (wd_hbm.at[heads], w_v.at[heads, :, BW:]),
            (cot_hbm.at[:, cols], cot_v.at[:, cols]),
        )
        return [pltpu.make_async_copy(s, d, in_sem.at[g, i]) for i, (s, d) in enumerate(pairs)]

    for g in range(GROUPS):
        for c in fetch(g):
            c.start()

    barrier = pltpu.get_barrier_semaphore()

    def hello(i, carry):
        pl.semaphore_signal(
            barrier,
            inc=1,
            device_id={"seq": lax.rem(me + i, SEQ_DEVICES)},
            device_id_type=MESH,
        )
        return carry

    lax.fori_loop(1, SEQ_DEVICES, hello, 0)

    seg = lax.broadcasted_iota(jnp.int32, (8, BW), 0)
    first = me * ROWS + seg * STEPS
    starts = [jnp.int32(0)]
    for j in range(DOCS - 1):
        starts.append(starts[-1] + docs_ref[j])
    for k in range(STEPS):
        hit = first + k == starts[0]
        for j in range(1, DOCS):
            hit = hit | (first + k == starts[j])
        reset_s[8 * k : 8 * k + 8, :] = jnp.where(hit, RESET, 0.0)
    logits = logit_ref[...]
    e = jnp.exp(-jnp.abs(logits))
    series = e * (1.0 + e * (-1 / 2 + e * (1 / 3 + e * (-1 / 4 + e * (1 / 5 + e * (-1 / 6))))))
    soft = jnp.maximum(logits, 0.0) + jnp.where(e < 0.0625, series, jnp.log(1.0 + e))
    k8_s[...] = -DECAY_SCALE * soft

    def send_tile(src, dst, send_sem, recv_sem, to, n=8):
        @pl.when(to != me)
        def _():
            pltpu.make_async_remote_copy(
                src_ref=src.at[to, 0:n],
                dst_ref=dst.at[me, 0:n],
                send_sem=send_sem,
                recv_sem=recv_sem,
                device_id={"seq": to},
                device_id_type=MESH,
            ).start()

    def wait_tiles(buf, sem, n=8, count=SEQ_DEVICES - 1):
        view = buf.at[pl.ds(0, count), 0:n]
        pltpu.make_async_copy(view, view, sem).wait()

    def lanes(h):
        return pl.ds(pl.multiple_of(h * BW, BW), BW)

    def gate_dots(h, in_s):
        sl = lanes(h)

        @pl.when((lax.rem(h, gh) == 0) & (h < HEADS - gh))
        def _():
            for c in fetch(h // gh):
                c.wait()

        xb = act_v[:, sl]
        for t, v in enumerate((xb.astype(F32), cot_v[:, sl].astype(F32), dot(xb, w_v[h]))):
            for i in range(v.shape[1] // ROWS):
                in_s[2 * t + i] = v[:, i * ROWS : (i + 1) * ROWS]

    def local_maps(h, in_s):
        sl = lanes(h)
        bi, bd = bi_ref[:, sl], bd_ref[:, sl]
        k8 = k8_s[:, sl] * LOG2E
        prod = jnp.ones((8, BW), F32)
        fwd = jnp.zeros((8, BW), F32)
        bwd = jnp.zeros((8, BW), F32)
        for k in range(STEPS):
            r = slice(8 * k, 8 * k + 8)
            tokens = pl.ds(k, 8, stride=STEPS)
            xk, ct, gi, gd = [
                jnp.concatenate([in_s[t, tokens, :], in_s[t + 1, tokens, :]], axis=1)
                for t in range(0, 8, 2)
            ]
            cotp[h, r, :] = ct
            ig = recip(1.0 + jnp.exp2((gi + bi) * -LOG2E))
            dg = recip(1.0 + jnp.exp2((gd + bd) * -LOG2E))
            ld = dg * k8 + reset_s[r, :]
            f = jnp.exp2(ld)
            th = jnp.tanh(ld * -LN2)
            comp = th + th * (f * f)
            root = lax.rsqrt(jnp.maximum(comp, TINY))
            a = ig * (comp * root)
            p = xk * a
            fac[h, r, :] = f
            psh[h, r, :] = p
            coef[h, r, :] = a
            quo[h, r, :] = f * (xk * ig) * jnp.minimum(root, ROOT_LIMIT)
            gin[h, r, :] = p * (1.0 - ig)
            dgate[h, r, :] = dg
            fwd = f * fwd + p
            prod = prod * f
            bwd = bwd + prod * ct
        fa, ba = prod, prod
        for d in (1, 2, 4):
            later = seg >= d
            fwd = jnp.where(later, fa * pltpu.roll(fwd, d, 0) + fwd, fwd)
            fa = jnp.where(later, fa * pltpu.roll(fa, d, 0), fa)
            earlier = seg < 8 - d
            bwd = jnp.where(earlier, ba * pltpu.roll(bwd, 8 - d, 0) + bwd, bwd)
            ba = jnp.where(earlier, ba * pltpu.roll(ba, 8 - d, 0), ba)
        whole = tile_of((fa[7:8], fwd[7:8], bwd[0:1]))
        seg_s[h, 0] = jnp.where(seg == 0, 1.0, pltpu.roll(fa, 1, 0))
        seg_s[h, 1] = jnp.where(seg == 0, 0.0, pltpu.roll(fwd, 1, 0))
        seg_s[h, 2] = jnp.where(seg == 7, 1.0, pltpu.roll(ba, 7, 0))
        seg_s[h, 3] = jnp.where(seg == 7, 0.0, pltpu.roll(bwd, 7, 0))
        for half in range(2):
            map_send[2 * h + half] = whole[:, half * ROWS : (half + 1) * ROWS]

    def share(h):
        for half in range(2):
            to = 2 * h + half

            @pl.when(to == me)
            def _():
                map_recv[me] = map_send[me]

            send_tile(map_send, map_recv, small_sem.at[0], small_sem.at[1], to, 3)

    def act_copy(d, k):
        yd = lax.rem(y + d, RING_Y)
        wide = gw // 2
        src = pl.ds(pl.multiple_of(yd * gw + k * wide, wide), wide)
        return pltpu.make_async_remote_copy(
            src_ref=act_v.at[:, src],
            dst_ref=act_all.at[d, :, pl.ds(k * wide, wide)],
            send_sem=act_ss.at[d, k],
            recv_sem=act_rs.at[d, k],
            device_id={"seq": yd * RING_Z + z},
            device_id_type=MESH,
        )

    def two_heads(i, carry):
        gate_dots(2 * i + 1, in_b)
        local_maps(2 * i, in_a)
        gate_dots(2 * i + 2 - (2 * i + 2) // HEADS, in_a)
        local_maps(2 * i + 1, in_b)
        return carry

    def two_heads_and_share(i, carry):
        two_heads(i, carry)
        for k in range(2):
            share(2 * i + k - HEADS // 2)
            share(2 * i + k)
        return carry

    gate_dots(0, in_a)
    lax.fori_loop(0, HEADS // 4, two_heads, 0)
    pl.semaphore_wait(barrier, SEQ_DEVICES - 1)
    for c in fetch(GROUPS - 1):
        c.wait()
    for d, k in ACT_EARLY:
        act_copy(d, k).start()
    lax.fori_loop(HEADS // 4, HEADS // 2, two_heads_and_share, 0)

    wait_tiles(map_recv, small_sem.at[1], 3)
    hid = jnp.zeros((1, ROWS), F32)
    for s in range(SEQ_DEVICES):
        rep_send[s, 0:1, :] = hid
        hid = map_recv[s, 0:1, :] * hid + map_recv[s, 1:2, :]
    back = jnp.zeros((1, ROWS), F32)
    for s in reversed(range(SEQ_DEVICES)):
        rep_send[s, 1:2, :] = back
        back = map_recv[s, 0:1, :] * back + map_recv[s, 2:3, :]
    rep_recv[me, 0:2] = rep_send[me, 0:2]

    zp, odd = z // 2, lax.rem(z, 2)

    def turns(j, parity):
        return (2, 1 + 2 * parity, 3 - 2 * parity, 0)[j]

    def reply(j, i, carry):
        parity = lax.rem(i, 2)
        tz = 2 * lax.rem(zp + RING_Z // 2 - turns(j, parity), RING_Z // 2) + parity
        to = i // 2 * RING_Z + tz

        @pl.when(to != me)
        def _():
            pltpu.make_async_remote_copy(
                src_ref=rep_send.at[to, 0:2],
                dst_ref=rep_recv.at[me, 0:2],
                send_sem=small_sem.at[2],
                recv_sem=rep_rs.at[j],
                device_id={"seq": to},
                device_id_type=MESH,
            ).start()

        return carry

    for j in range(4):
        lax.fori_loop(0, 2 * RING_Y, functools.partial(reply, j), 0)
    for d, k in ACT_LATE:
        act_copy(d, k).start()

    def chains(h):
        sl = lanes(h)
        t0, t1 = rep_recv[2 * h], rep_recv[2 * h + 1]
        hin = jnp.concatenate([t0[0:1], t1[0:1]], axis=1)
        cin = jnp.concatenate([t0[1:2], t1[1:2]], axis=1)
        hid = seg_s[h, 0] * hin + seg_s[h, 1]
        c = seg_s[h, 2] * cin + seg_s[h, 3]
        for k in reversed(range(STEPS)):
            r = slice(8 * k, 8 * k + 8)
            u = cotp[h, r, :] + c
            u_s[r, :] = u
            c = fac[h, r, :] * u
        k8 = k8_s[:, sl]
        sum_i = jnp.zeros((8, BW), F32)
        sum_d = jnp.zeros((8, BW), F32)
        sum_l = jnp.zeros((8, BW), F32)
        for k in range(STEPS):
            r = slice(8 * k, 8 * k + 8)
            u = u_s[r, :]
            f = fac[h, r, :]
            dg = dgate[h, r, :]
            dl = f * u * (hid - quo[h, r, :]) * dg
            pd = k8 * dl * (1.0 - dg)
            pi = u * gin[h, r, :]
            hid = f * hid + psh[h, r, :]
            sum_i = sum_i + pi
            sum_d = sum_d + pd
            sum_l = sum_l + dl
            tokens = pl.ds(k, 8, stride=STEPS)
            du = u * coef[h, r, :]
            for t in range(2):
                cols = slice(t * ROWS, (t + 1) * ROWS)
                stage[t, tokens, :] = pi[:, cols]
                stage[2 + t, tokens, :] = pd[:, cols]
                stage[4 + t, tokens, :] = hid[:, cols]
                direct[2 * h + t, tokens, :] = du[:, cols]
        both = jnp.concatenate([stage[t] for t in range(4)], axis=1).astype(BF16)
        low_s[h] = both
        states_v[:, sl] = jnp.concatenate([stage[4], stage[5]], axis=1).astype(BF16)
        wg = dot(act_v[:, sl], both[:, YZ:], ((0,), (0,)))
        part[2 * h] = wg[:ROWS]
        part[2 * h + 1] = wg[ROWS:]
        sums = tile_of(
            [jnp.sum(s, axis=0, keepdims=True) for s in (sum_i, sum_d, sum_l)]
        )
        for half in range(2):
            to = 2 * h + half
            piece = sums[:, half * ROWS : (half + 1) * ROWS]
            bias_send[to] = piece

            @pl.when(to == me)
            def _():
                bias_recv[me] = piece

            send_tile(bias_send, bias_recv, small_sem.at[4], small_sem.at[5], to)

    def group_of(j):
        return lax.rem(zp + turns(j, odd), RING_Z // 2)

    def make_group(j):
        q = group_of(j)
        wait_tiles(rep_recv, rep_rs.at[j], 2, 2 * RING_Y - (j == 3))

        def one(i, carry):
            d = lax.rem(i + 2, RING_Y)
            yd = lax.rem(y + d, RING_Y)
            h = yd * (RING_Z // 2) + q
            chains(h)

            @pl.when(d != 0)
            def _():
                pltpu.make_async_remote_copy(
                    src_ref=low_s.at[h, :, pl.ds(0, YZ)],
                    dst_ref=low_all.at[q, d],
                    send_sem=low_ss.at[j, d],
                    recv_sem=low_rs.at[j, d],
                    device_id={"seq": yd * RING_Z + z},
                    device_id_type=MESH,
                ).start()

            return carry

        lax.fori_loop(0, RING_Y, one, 0)

    def finish(h, carry):
        sl = lanes(h)
        mine = jnp.concatenate([direct[2 * h], direct[2 * h + 1]], axis=1)
        ig = mine + dot(low_s[h], w_v[h], ((1,), (1,)))
        grads_v[:, sl] = ig.astype(BF16)
        return carry

    def finish_quarter(i):
        lax.fori_loop(i * HEADS // 4, (i + 1) * HEADS // 4, finish, 0)

    def half(p):
        return slice(p * HALF, (p + 1) * HALF)

    def landed(buf, sem):
        pltpu.make_async_copy(buf, buf, sem).wait()

    def z_at(off):
        return lax.rem(z + off + RING_Z, RING_Z)

    def y_at(off):
        return lax.rem(y + off + RING_Y, RING_Y)

    sends = []

    def launch(src, dst, ssem, rsem, ty, tz):
        copy = pltpu.make_async_remote_copy(
            src_ref=src,
            dst_ref=dst,
            send_sem=ssem,
            recv_sem=rsem,
            device_id={"seq": ty * RING_Z + tz},
            device_id_type=MESH,
        )
        copy.start()
        sends.append(copy)
        return copy

    z1, z2, y2 = {}, {}, {}

    def z1_send(c, i):
        p, way, hops = Z_CHAINS[c]
        n = Z_SLOT[(c, i)]
        zd = z_at(way * (hops - i))
        if i:
            z1[(c, i - 1)].wait_recv()
        for d in range(RING_Y):
            v = part[y_at(d) * RING_Z + zd, half(p), :]
            if i:
                v = v + z1r[n - 1, d].astype(F32)
            z1s[n, d] = v.astype(BF16)
        z1[(c, i)] = launch(z1s.at[n], z1r.at[n], z1_ss.at[n], z1_rs.at[n], y, z_at(way))

    def last_of(p):
        return [Z_SLOT[(c, ch[2] - 1)] for c, ch in enumerate(Z_CHAINS) if ch[0] == p]

    def z1_fin():
        for c, (p, way, hops) in enumerate(Z_CHAINS):
            z1[(c, hops - 1)].wait_recv()
        for p in range(2):
            n, m = last_of(p)
            for d in range(RING_Y):
                v = part[y_at(d) * RING_Z + z, half(p), :] + (
                    z1r[n, d].astype(F32) + z1r[m, d].astype(F32)
                )
                if d:
                    y2s[d, half(p), :] = v.astype(BF16)
                else:
                    part[me, half(p), :] = v
        for d in (2, 1, 3):
            y2[d] = launch(y2s.at[d], y2r.at[d], y2_ss.at[d], y2_rs.at[d], y_at(d), z)

    def product(j):
        q = group_of(j)
        if j == 0:
            for d, k in ACT_EARLY + ACT_LATE:
                act_copy(d, k).wait_recv()
        for d in range(1, RING_Y):
            landed(low_all.at[q, d], low_rs.at[j, d])
        h = y * (RING_Z // 2) + q
        acts = [act_v[:, lanes(h)]] + [act_all[d, :, lanes(q)] for d in range(1, RING_Y)]
        lows = [low_s[h, :, :YZ]] + [low_all[q, d] for d in range(1, RING_Y)]
        acts, lows = jnp.concatenate(acts, axis=0), jnp.concatenate(lows, axis=0)
        wg = dot(acts, lows, ((0,), (0,)))
        prods[2 * q] = wg[:ROWS]
        prods[2 * q + 1] = wg[ROWS:]

    def z2_step(distance):
        for c, (p, way, hops) in enumerate(Z_CHAINS):
            i = hops - distance
            if i < 0:
                continue
            n = Z_SLOT[(c, i)]
            if i:
                z2[(c, i - 1)].wait_recv()
            v = prods[z_at(way * distance), half(p), :]
            if i:
                v = v + z2r[n - 1].astype(F32)
            z2s[n] = v.astype(BF16)
            z2[(c, i)] = launch(z2s.at[n], z2r.at[n], z2_ss.at[n], z2_rs.at[n], y, z_at(way))

    def z1_sends(*which):
        for c, i in which:
            z1_send(c, i)

    make_group(0)
    z1_sends((0, 0), (3, 0))
    make_group(1)
    z1_sends((1, 0), (2, 0))
    make_group(2)
    z1_sends((0, 1), (3, 1))
    make_group(3)
    z1_sends((1, 1), (2, 1))
    product(0)
    z2_step(4)
    z1_sends((0, 2), (3, 2))
    finish_quarter(0)
    z1_sends((1, 2), (2, 2), (0, 3), (3, 3))
    product(1)
    z2_step(3)
    finish_quarter(1)
    z1_fin()
    finish_quarter(2)
    product(2)
    z2_step(2)
    finish_quarter(3)
    product(3)
    z2_step(1)

    wait_tiles(bias_recv, small_sem.at[5])
    total = bias_recv[0]
    for s in range(1, SEQ_DEVICES):
        total = total + bias_recv[s]
    mine = logit_ref[:, pl.ds(pl.multiple_of(me * ROWS, ROWS), ROWS)]
    vec_ref[0:1, :] = total[0:1]
    vec_ref[1:2, :] = total[1:2]
    vec_ref[2:3, :] = total[2:3] * (-DECAY_SCALE / (1.0 + jnp.exp(-mine)))

    for d in range(1, RING_Y):
        y2[d].wait_recv()
    rest = part[me] + (y2r[1].astype(F32) + y2r[2].astype(F32) + y2r[3].astype(F32))
    wgd_ref[:, 2 * BW - YZ :] = rest
    for c, (p, way, hops) in enumerate(Z_CHAINS):
        z2[(c, hops - 1)].wait_recv()
    for p in range(2):
        n, m = last_of(p)
        done = prods[z, half(p), :] + (z2r[n].astype(F32) + z2r[m].astype(F32))
        wgi_ref[half(p), :] = done[:, :BW]
        wgd_ref[half(p), : YZ - BW] = done[:, BW:]

    for s in sends:
        s.wait_send()
    for d, k in ACT_EARLY + ACT_LATE:
        act_copy(d, k).wait_send()
    for d in range(1, RING_Y):
        for k in range(RING_Z // 2):
            landed(low_all.at[k, d], low_ss.at[k, d])
    wait_tiles(map_send, small_sem.at[0], 3)
    wait_tiles(rep_send, small_sem.at[2], 2)
    wait_tiles(bias_send, small_sem.at[4])


def hand_over(*refs):
    ins, outs, sem = refs[:5], refs[5:12], refs[12]
    pairs = list(zip(ins[:4], outs[:4]))
    pairs += [(ins[4].at[pl.ds(i, 1)], outs[4 + i]) for i in range(3)]
    copies = [pltpu.make_async_copy(s, d, sem.at[i]) for i, (s, d) in enumerate(pairs)]
    for c in copies:
        c.start()
    for c in copies:
        c.wait()


def on_device(act, wi, wd, bi, bd, logits, docs, cot):
    any_spec = pl.BlockSpec(memory_space=pl.ANY)
    vmem = pl.BlockSpec(memory_space=pltpu.VMEM)
    smem = pl.BlockSpec(memory_space=pltpu.SMEM)
    chunk = (HEADS, ROWS, BW)
    scratch = [
        pltpu.VMEM((ROWS, WIDTH), BF16),
        pltpu.VMEM((ROWS, WIDTH), BF16),
        pltpu.VMEM((HEADS, BW, 2 * BW), BF16),
        *[pltpu.VMEM(chunk, F32)] * 7,
        pltpu.VMEM((2 * HEADS, ROWS, ROWS), F32),
        pltpu.VMEM((HEADS, ROWS, 2 * BW), BF16),
        pltpu.VMEM((ROWS, BW), F32),
        pltpu.VMEM((6, ROWS, ROWS), F32),
        pltpu.VMEM((ROWS, BW), F32),
        pltpu.VMEM((1, WIDTH), F32),
        pltpu.VMEM((HEADS, 4, 8, BW), F32),
        pltpu.VMEM((SEQ_DEVICES, ROWS, ZY), F32),
        pltpu.VMEM((RING_Z, ROWS, YZ), F32),
        pltpu.VMEM((8, ROWS, ROWS), F32),
        pltpu.VMEM((8, ROWS, ROWS), F32),
        pltpu.VMEM((RING_Y, ROWS, WIDTH // RING_Y), BF16),
        pltpu.VMEM((RING_Z // 2, RING_Y, ROWS, YZ), BF16),
    ]
    scratch += [pltpu.VMEM((SEQ_DEVICES, 8, ROWS), F32) for _ in range(6)]
    for shape in (
        (Z_COUNT, RING_Y, HALF, ZY),
        (Z_COUNT, HALF, YZ),
        (RING_Y, ROWS, ZY),
    ):
        scratch += [pltpu.VMEM(shape, BF16), pltpu.VMEM(shape, BF16)]
    scratch += [
        pltpu.SemaphoreType.DMA((GROUPS, 4)),
        pltpu.SemaphoreType.DMA((6,)),
    ]
    quads = (RING_Z // 2, RING_Y)
    for shape in ((Z_COUNT,), (Z_COUNT,), (RING_Y,), (RING_Y, 2), quads):
        scratch += [pltpu.SemaphoreType.DMA(shape), pltpu.SemaphoreType.DMA(shape)]
    scratch.append(pltpu.SemaphoreType.DMA((4,)))
    results = pl.pallas_call(
        kernel,
        out_shape=(
            pltpu.VMEM((ROWS, WIDTH), BF16),
            pltpu.VMEM((ROWS, WIDTH), BF16),
            pltpu.VMEM((ROWS, BW), F32),
            pltpu.VMEM((ROWS, BW), F32),
            pltpu.VMEM((8, ROWS), F32),
        ),
        in_specs=[smem, any_spec, any_spec, any_spec, vmem, vmem, vmem, any_spec],
        out_specs=(vmem,) * 5,
        scratch_shapes=scratch,
        compiler_params=pltpu.CompilerParams(
            collective_id=0, has_side_effects=True, vmem_limit_bytes=60 * 1024 * 1024
        ),
    )(
        docs,
        act,
        wi,
        wd,
        bi.reshape(1, WIDTH),
        bd.reshape(1, WIDTH),
        logits.reshape(1, WIDTH),
        cot,
    )
    results = [pltpu.with_memory_space_constraint(r, pltpu.VMEM) for r in results]
    outs = pl.pallas_call(
        hand_over,
        out_shape=[jax.ShapeDtypeStruct(a.shape, a.dtype) for a in results[:4]]
        + [jax.ShapeDtypeStruct((1, ROWS), F32)] * 3,
        in_specs=[vmem] * 5,
        out_specs=[any_spec] * 7,
        scratch_shapes=[pltpu.SemaphoreType.DMA((7,))],
    )(*results)
    return (*outs[:4], *(v.reshape(ROWS) for v in outs[4:]))


def solution(mesh):
    rows = P(("grp", "seq"), None)
    flat = P(("grp", "seq"))
    return jax.shard_map(
        on_device,
        mesh=mesh,
        in_specs=(rows, P(), P(), P(), P(), P(), P("grp"), rows),
        out_specs=(rows, rows, rows, rows, flat, flat, flat),
        check_vma=False,
    )
```

```python
import functools

import jax
import jax.numpy as jnp
from jax import lax
from jax.experimental import pallas as pl
from jax.experimental.pallas import tpu as pltpu
from jax.sharding import PartitionSpec as P

ROWS = 128
WIDTH = 4096
HEADS = 16
BW = 256
DOCS = 6
RING_Y = 4
RING_Z = 8
SEQ_DEVICES = RING_Y * RING_Z
STEPS = 16
GROUPS = 4
ZY = 128
YZ = 2 * BW - ZY
PIECES = 2
PIECE = ROWS // PIECES
DECAY_SCALE = 8.0
ROOT_LIMIT = 2000.0
TINY = 1.2e-38
MESH = pl.DeviceIdType.MESH
F32 = jnp.float32
BF16 = jnp.bfloat16

Z_CHAINS = tuple((p, way, 3 + ((p % 2 == 0) == (way > 0))) for p in range(PIECES) for way in (1, -1))
LOG2E = 1.4426950408889634
LN2 = 0.6931471805599453
RESET = -1e4
ACT_EARLY, ACT_NEXT, ACT_LATE = (0,), (1, 2), (3,)


def slots_of(chains):
    table, count = {}, 0
    for c, (_, _, hops) in enumerate(chains):
        for i in range(hops):
            table[(c, i)] = count
            count += 1
    return table, count


Z_SLOT, Z_COUNT = slots_of(Z_CHAINS)


def dot(a, b, dims=((1,), (0,))):
    return lax.dot_general(a, b, (dims, ((), ())), preferred_element_type=F32)


def recip(x):
    return pltpu.reciprocal(x, approx=True)


def tile_of(rows):
    pad = jnp.zeros((8 - len(rows), rows[0].shape[1]), F32)
    return jnp.concatenate(list(rows) + [pad], axis=0)


def kernel(
    docs_ref,
    act_hbm,
    wi_hbm,
    wd_hbm,
    bi_ref,
    bd_ref,
    logit_ref,
    cot_hbm,
    states_v,
    grads_v,
    wgi_ref,
    wgd_ref,
    vec_ref,
    act_v,
    cot_v,
    w_v,
    cotp,
    fac,
    psh,
    coef,
    quo,
    gin,
    dgate,
    direct,
    low_s,
    u_s,
    stage,
    reset_s,
    k8_s,
    seg_s,
    part,
    prods,
    in_a,
    in_b,
    act_all,
    low_all,
    map_send,
    map_recv,
    rep_send,
    rep_recv,
    bias_send,
    bias_recv,
    z1s,
    z1r,
    z2s,
    z2r,
    y2s,
    y2r,
    in_sem,
    small_sem,
    z1_ss,
    z1_rs,
    z2_ss,
    z2_rs,
    y2_ss,
    y2_rs,
    act_ss,
    act_rs,
    low_ss,
    low_rs,
    rep_rs,
):
    me = lax.axis_index("seq")
    y, z = me // RING_Z, lax.rem(me, RING_Z)

    gw = WIDTH // GROUPS
    gh = HEADS // GROUPS

    def fetch(g):
        cols = pl.ds(pl.multiple_of(g * gw, gw), gw)
        heads = pl.ds(g * gh, gh)
        pairs = (
            (act_hbm.at[:, cols], act_v.at[:, cols]),
            (wi_hbm.at[heads], w_v.at[heads, :, 0:BW]),
            (wd_hbm.at[heads], w_v.at[heads, :, BW:]),
            (cot_hbm.at[:, cols], cot_v.at[:, cols]),
        )
        return [pltpu.make_async_copy(s, d, in_sem.at[g, i]) for i, (s, d) in enumerate(pairs)]

    for g in range(GROUPS):
        for c in fetch(g):
            c.start()

    barrier = pltpu.get_barrier_semaphore()

    def hello(i, carry):
        pl.semaphore_signal(
            barrier,
            inc=1,
            device_id={"seq": lax.rem(me + i, SEQ_DEVICES)},
            device_id_type=MESH,
        )
        return carry

    lax.fori_loop(1, SEQ_DEVICES, hello, 0)

    seg = lax.broadcasted_iota(jnp.int32, (8, BW), 0)
    first = me * ROWS + seg * STEPS
    starts = [jnp.int32(0)]
    for j in range(DOCS - 1):
        starts.append(starts[-1] + docs_ref[j])
    for k in range(STEPS):
        hit = first + k == starts[0]
        for j in range(1, DOCS):
            hit = hit | (first + k == starts[j])
        reset_s[8 * k : 8 * k + 8, :] = jnp.where(hit, RESET, 0.0)
    logits = logit_ref[...]
    e = jnp.exp(-jnp.abs(logits))
    series = e * (1.0 + e * (-1 / 2 + e * (1 / 3 + e * (-1 / 4 + e * (1 / 5 + e * (-1 / 6))))))
    soft = jnp.maximum(logits, 0.0) + jnp.where(e < 0.0625, series, jnp.log(1.0 + e))
    k8_s[...] = -DECAY_SCALE * soft

    def send_tile(src, dst, send_sem, recv_sem, to, n=8):
        @pl.when(to != me)
        def _():
            pltpu.make_async_remote_copy(
                src_ref=src.at[to, 0:n],
                dst_ref=dst.at[me, 0:n],
                send_sem=send_sem,
                recv_sem=recv_sem,
                device_id={"seq": to},
                device_id_type=MESH,
            ).start()

    def wait_tiles(buf, sem, n=8, count=SEQ_DEVICES - 1):
        view = buf.at[pl.ds(0, count), 0:n]
        pltpu.make_async_copy(view, view, sem).wait()

    def lanes(h):
        return pl.ds(pl.multiple_of(h * BW, BW), BW)

    def gate_dots(h, in_s):
        sl = lanes(h)

        @pl.when((lax.rem(h, gh) == 0) & (h < HEADS - gh))
        def _():
            for c in fetch(h // gh):
                c.wait()

        xb = act_v[:, sl]
        for t, v in enumerate((xb.astype(F32), cot_v[:, sl].astype(F32), dot(xb, w_v[h]))):
            for i in range(v.shape[1] // ROWS):
                in_s[2 * t + i] = v[:, i * ROWS : (i + 1) * ROWS]

    def local_maps(h, in_s):
        sl = lanes(h)
        bi, bd = bi_ref[:, sl], bd_ref[:, sl]
        k8 = k8_s[:, sl] * LOG2E
        prod = jnp.ones((8, BW), F32)
        fwd = jnp.zeros((8, BW), F32)
        bwd = jnp.zeros((8, BW), F32)
        for k in range(STEPS):
            r = slice(8 * k, 8 * k + 8)
            tokens = pl.ds(k, 8, stride=STEPS)
            xk, ct, gi, gd = [
                jnp.concatenate([in_s[t, tokens, :], in_s[t + 1, tokens, :]], axis=1)
                for t in range(0, 8, 2)
            ]
            cotp[h, r, :] = ct
            ig = recip(1.0 + jnp.exp2((gi + bi) * -LOG2E))
            dg = recip(1.0 + jnp.exp2((gd + bd) * -LOG2E))
            ld = dg * k8 + reset_s[r, :]
            f = jnp.exp2(ld)
            th = jnp.tanh(ld * -LN2)
            comp = th + th * (f * f)
            root = lax.rsqrt(jnp.maximum(comp, TINY))
            a = ig * (comp * root)
            p = xk * a
            fac[h, r, :] = f
            psh[h, r, :] = p
            coef[h, r, :] = a
            quo[h, r, :] = f * (xk * ig) * jnp.minimum(root, ROOT_LIMIT)
            gin[h, r, :] = p * (1.0 - ig)
            dgate[h, r, :] = dg
            fwd = f * fwd + p
            prod = prod * f
            bwd = bwd + prod * ct
        fa, ba = prod, prod
        for d in (1, 2, 4):
            later = seg >= d
            fwd = jnp.where(later, fa * pltpu.roll(fwd, d, 0) + fwd, fwd)
            fa = jnp.where(later, fa * pltpu.roll(fa, d, 0), fa)
            earlier = seg < 8 - d
            bwd = jnp.where(earlier, ba * pltpu.roll(bwd, 8 - d, 0) + bwd, bwd)
            ba = jnp.where(earlier, ba * pltpu.roll(ba, 8 - d, 0), ba)
        whole = tile_of((fa[7:8], fwd[7:8], bwd[0:1]))
        seg_s[h, 0] = jnp.where(seg == 0, 1.0, pltpu.roll(fa, 1, 0))
        seg_s[h, 1] = jnp.where(seg == 0, 0.0, pltpu.roll(fwd, 1, 0))
        seg_s[h, 2] = jnp.where(seg == 7, 1.0, pltpu.roll(ba, 7, 0))
        seg_s[h, 3] = jnp.where(seg == 7, 0.0, pltpu.roll(bwd, 7, 0))
        for half in range(2):
            map_send[2 * h + half] = whole[:, half * ROWS : (half + 1) * ROWS]

    def share(h):
        for half in range(2):
            to = 2 * h + half

            @pl.when(to == me)
            def _():
                map_recv[me] = map_send[me]

            send_tile(map_send, map_recv, small_sem.at[0], small_sem.at[1], to, 3)

    zp, odd = z // 2, lax.rem(z, 2)

    def turns(j, parity):
        return (2, 1 + 2 * parity, 3 - 2 * parity, 0)[j]

    def group_of(j):
        return lax.rem(zp + turns(j, odd), RING_Z // 2)

    def act_copy(d, j):
        yd, q = lax.rem(y + d, RING_Y), group_of(j)
        return pltpu.make_async_remote_copy(
            src_ref=act_v.at[:, lanes(yd * (RING_Z // 2) + q)],
            dst_ref=act_all.at[d, :, lanes(q)],
            send_sem=act_ss.at[d, j],
            recv_sem=act_rs.at[d, j],
            device_id={"seq": yd * RING_Z + z},
            device_id_type=MESH,
        )

    def act_send(groups):
        for j in groups:
            for d in (2, 3, 1):
                act_copy(d, j).start()

    def two_heads(i, carry):
        gate_dots(2 * i + 1, in_b)
        local_maps(2 * i, in_a)
        gate_dots(2 * i + 2 - (2 * i + 2) // HEADS, in_a)
        local_maps(2 * i + 1, in_b)
        return carry

    def two_heads_and_share(i, carry):
        two_heads(i, carry)
        for k in range(2):
            share(2 * i + k - HEADS // 2)
            share(2 * i + k)
        return carry

    gate_dots(0, in_a)
    lax.fori_loop(0, HEADS // 4, two_heads, 0)
    pl.semaphore_wait(barrier, SEQ_DEVICES - 1)
    for c in fetch(GROUPS - 1):
        c.wait()
    act_send(ACT_EARLY)
    lax.fori_loop(HEADS // 4, HEADS // 2, two_heads_and_share, 0)

    wait_tiles(map_recv, small_sem.at[1], 3)
    hid = jnp.zeros((1, ROWS), F32)
    for s in range(SEQ_DEVICES):
        rep_send[s, 0:1, :] = hid
        hid = map_recv[s, 0:1, :] * hid + map_recv[s, 1:2, :]
    back = jnp.zeros((1, ROWS), F32)
    for s in reversed(range(SEQ_DEVICES)):
        rep_send[s, 1:2, :] = back
        back = map_recv[s, 0:1, :] * back + map_recv[s, 2:3, :]
    rep_recv[me, 0:2] = rep_send[me, 0:2]

    def reply(j, i, carry):
        parity = lax.rem(i, 2)
        tz = 2 * lax.rem(zp + RING_Z // 2 - turns(j, parity), RING_Z // 2) + parity
        to = i // 2 * RING_Z + tz

        @pl.when(to != me)
        def _():
            pltpu.make_async_remote_copy(
                src_ref=rep_send.at[to, 0:2],
                dst_ref=rep_recv.at[me, 0:2],
                send_sem=small_sem.at[2],
                recv_sem=rep_rs.at[j],
                device_id={"seq": to},
                device_id_type=MESH,
            ).start()

        return carry

    for j in range(4):
        lax.fori_loop(0, 2 * RING_Y, functools.partial(reply, j), 0)
    act_send(ACT_NEXT)

    def chains(h):
        sl = lanes(h)
        t0, t1 = rep_recv[2 * h], rep_recv[2 * h + 1]
        hin = jnp.concatenate([t0[0:1], t1[0:1]], axis=1)
        cin = jnp.concatenate([t0[1:2], t1[1:2]], axis=1)
        hid = seg_s[h, 0] * hin + seg_s[h, 1]
        c = seg_s[h, 2] * cin + seg_s[h, 3]
        for k in reversed(range(STEPS)):
            r = slice(8 * k, 8 * k + 8)
            u = cotp[h, r, :] + c
            u_s[r, :] = u
            c = fac[h, r, :] * u
        k8 = k8_s[:, sl]
        sum_i = jnp.zeros((8, BW), F32)
        sum_d = jnp.zeros((8, BW), F32)
        sum_l = jnp.zeros((8, BW), F32)
        for k in range(STEPS):
            r = slice(8 * k, 8 * k + 8)
            u = u_s[r, :]
            f = fac[h, r, :]
            dg = dgate[h, r, :]
            dl = f * u * (hid - quo[h, r, :]) * dg
            pd = k8 * dl * (1.0 - dg)
            pi = u * gin[h, r, :]
            hid = f * hid + psh[h, r, :]
            sum_i = sum_i + pi
            sum_d = sum_d + pd
            sum_l = sum_l + dl
            tokens = pl.ds(k, 8, stride=STEPS)
            du = u * coef[h, r, :]
            for t in range(2):
                cols = slice(t * ROWS, (t + 1) * ROWS)
                stage[t, tokens, :] = pi[:, cols]
                stage[2 + t, tokens, :] = pd[:, cols]
                stage[4 + t, tokens, :] = hid[:, cols]
                direct[2 * h + t, tokens, :] = du[:, cols]
        both = jnp.concatenate([stage[t] for t in range(4)], axis=1).astype(BF16)
        low_s[h] = both
        states_v[:, sl] = jnp.concatenate([stage[4], stage[5]], axis=1).astype(BF16)
        wg = dot(act_v[:, sl], both[:, YZ:], ((0,), (0,)))
        part[2 * h] = wg[:ROWS]
        part[2 * h + 1] = wg[ROWS:]
        sums = tile_of(
            [jnp.sum(s, axis=0, keepdims=True) for s in (sum_i, sum_d, sum_l)]
        )
        for half in range(2):
            to = 2 * h + half
            piece = sums[:, half * ROWS : (half + 1) * ROWS]
            bias_send[to] = piece

            @pl.when(to == me)
            def _():
                bias_recv[me] = piece

            send_tile(bias_send, bias_recv, small_sem.at[4], small_sem.at[5], to)

    def low_copy(j, d):
        q = group_of(j)
        yd = lax.rem(y + d, RING_Y)
        return pltpu.make_async_remote_copy(
            src_ref=low_s.at[yd * (RING_Z // 2) + q, :, pl.ds(0, YZ)],
            dst_ref=low_all.at[q, d],
            send_sem=low_ss.at[j, d],
            recv_sem=low_rs.at[j, d],
            device_id={"seq": yd * RING_Z + z},
            device_id_type=MESH,
        )

    def make_group(j, send):
        q = group_of(j)
        wait_tiles(rep_recv, rep_rs.at[j], 2, 2 * RING_Y - (j == 3))

        def one(i, carry):
            d = lax.rem(i + 2, RING_Y)
            chains(lax.rem(y + d, RING_Y) * (RING_Z // 2) + q)

            if send:

                @pl.when(d != 0)
                def _():
                    low_copy(j, d).start()

            return carry

        lax.fori_loop(0, RING_Y, one, 0)

    def send_group(j):
        for d in (2, 3, 1):
            low_copy(j, d).start()

    def finish(h, carry):
        sl = lanes(h)
        mine = jnp.concatenate([direct[2 * h], direct[2 * h + 1]], axis=1)
        ig = mine + dot(low_s[h], w_v[h], ((1,), (1,)))
        grads_v[:, sl] = ig.astype(BF16)
        return carry

    def finish_quarter(i):
        lax.fori_loop(i * HEADS // 4, (i + 1) * HEADS // 4, finish, 0)

    def piece_of(p):
        return slice(p * PIECE, (p + 1) * PIECE)

    def z_at(off):
        return lax.rem(z + off + RING_Z, RING_Z)

    def y_at(off):
        return lax.rem(y + off + RING_Y, RING_Y)

    sends = []

    def launch(src, dst, ssem, rsem, ty, tz):
        copy = pltpu.make_async_remote_copy(
            src_ref=src,
            dst_ref=dst,
            send_sem=ssem,
            recv_sem=rsem,
            device_id={"seq": ty * RING_Z + tz},
            device_id_type=MESH,
        )
        copy.start()
        sends.append(copy)
        return copy

    z1, z2, y2 = {}, {}, {}

    def z1_send(c, i):
        p, way, hops = Z_CHAINS[c]
        n = Z_SLOT[(c, i)]
        zd = z_at(way * (hops - i))
        if i:
            z1[(c, i - 1)].wait_recv()
        for d in range(RING_Y):
            v = part[y_at(d) * RING_Z + zd, piece_of(p), :]
            if i:
                v = v + z1r[n - 1, d].astype(F32)
            z1s[n, d] = v.astype(BF16)
        z1[(c, i)] = launch(z1s.at[n], z1r.at[n], z1_ss.at[n], z1_rs.at[n], y, z_at(way))

    def last_of(p):
        return [Z_SLOT[(c, ch[2] - 1)] for c, ch in enumerate(Z_CHAINS) if ch[0] == p]

    def z1_fin():
        for c, (p, way, hops) in enumerate(Z_CHAINS):
            z1[(c, hops - 1)].wait_recv()
        for p in range(PIECES):
            n, m = last_of(p)
            for d in range(RING_Y):
                v = part[y_at(d) * RING_Z + z, piece_of(p), :] + (
                    z1r[n, d].astype(F32) + z1r[m, d].astype(F32)
                )
                if d:
                    y2s[d, piece_of(p), :] = v.astype(BF16)
                else:
                    part[me, piece_of(p), :] = v
        for d in (2, 1, 3):
            y2[d] = launch(y2s.at[d], y2r.at[d], y2_ss.at[d], y2_rs.at[d], y_at(d), z)

    def product(j):
        q = group_of(j)
        for d in range(1, RING_Y):
            act_copy(d, j).wait_recv()
            low_copy(j, d).wait_recv()
        h = y * (RING_Z // 2) + q
        acts = [act_v[:, lanes(h)]] + [act_all[d, :, lanes(q)] for d in range(1, RING_Y)]
        lows = [low_s[h, :, :YZ]] + [low_all[q, d] for d in range(1, RING_Y)]
        acts, lows = jnp.concatenate(acts, axis=0), jnp.concatenate(lows, axis=0)
        wg = dot(acts, lows, ((0,), (0,)))
        prods[2 * q] = wg[:ROWS]
        prods[2 * q + 1] = wg[ROWS:]

    def z2_step(distance):
        for c, (p, way, hops) in enumerate(Z_CHAINS):
            i = hops - distance
            if i < 0:
                continue
            n = Z_SLOT[(c, i)]
            if i:
                z2[(c, i - 1)].wait_recv()
            v = prods[z_at(way * distance), piece_of(p), :]
            if i:
                v = v + z2r[n - 1].astype(F32)
            z2s[n] = v.astype(BF16)
            z2[(c, i)] = launch(z2s.at[n], z2r.at[n], z2_ss.at[n], z2_rs.at[n], y, z_at(way))

    def z1_step(distance, hops=(4, 3)):
        for c, chain in enumerate(Z_CHAINS):
            if chain[2] in hops and chain[2] >= distance:
                z1_send(c, chain[2] - distance)

    make_group(0, True)
    z1_step(4)
    make_group(1, True)
    z1_step(3, (3,))
    make_group(2, False)
    z1_step(3, (4,))
    product(0)
    z2_step(4)
    send_group(2)
    make_group(3, False)
    z1_step(2)
    product(1)
    z2_step(3)
    act_send(ACT_LATE)
    send_group(3)
    finish_quarter(0)
    z1_step(1)
    finish_quarter(1)
    product(2)
    z2_step(2)
    finish_quarter(2)
    z1_fin()
    finish_quarter(3)
    product(3)
    z2_step(1)

    wait_tiles(bias_recv, small_sem.at[5])
    total = bias_recv[0]
    for s in range(1, SEQ_DEVICES):
        total = total + bias_recv[s]
    mine = logit_ref[:, pl.ds(pl.multiple_of(me * ROWS, ROWS), ROWS)]
    vec_ref[0:1, :] = total[0:1]
    vec_ref[1:2, :] = total[1:2]
    vec_ref[2:3, :] = total[2:3] * (-DECAY_SCALE / (1.0 + jnp.exp(-mine)))

    for d in range(1, RING_Y):
        y2[d].wait_recv()
    rest = part[me] + (y2r[1].astype(F32) + y2r[2].astype(F32) + y2r[3].astype(F32))
    wgd_ref[:, 2 * BW - YZ :] = rest
    for c, (p, way, hops) in enumerate(Z_CHAINS):
        z2[(c, hops - 1)].wait_recv()
    for p in range(PIECES):
        n, m = last_of(p)
        done = prods[z, piece_of(p), :] + (z2r[n].astype(F32) + z2r[m].astype(F32))
        wgi_ref[piece_of(p), :] = done[:, :BW]
        wgd_ref[piece_of(p), : YZ - BW] = done[:, BW:]

    for s in sends:
        s.wait_send()
    for d in range(1, RING_Y):
        for j in range(RING_Z // 2):
            act_copy(d, j).wait_send()
        for j in range(RING_Z // 2):
            low_copy(j, d).wait_send()
    wait_tiles(map_send, small_sem.at[0], 3)
    wait_tiles(rep_send, small_sem.at[2], 2)
    wait_tiles(bias_send, small_sem.at[4])


def hand_over(*refs):
    ins, outs, sem = refs[:5], refs[5:12], refs[12]
    pairs = list(zip(ins[:4], outs[:4]))
    pairs += [(ins[4].at[pl.ds(i, 1)], outs[4 + i]) for i in range(3)]
    copies = [pltpu.make_async_copy(s, d, sem.at[i]) for i, (s, d) in enumerate(pairs)]
    for c in copies:
        c.start()
    for c in copies:
        c.wait()


def on_device(act, wi, wd, bi, bd, logits, docs, cot):
    any_spec = pl.BlockSpec(memory_space=pl.ANY)
    vmem = pl.BlockSpec(memory_space=pltpu.VMEM)
    smem = pl.BlockSpec(memory_space=pltpu.SMEM)
    chunk = (HEADS, ROWS, BW)
    scratch = [
        pltpu.VMEM((ROWS, WIDTH), BF16),
        pltpu.VMEM((ROWS, WIDTH), BF16),
        pltpu.VMEM((HEADS, BW, 2 * BW), BF16),
        *[pltpu.VMEM(chunk, F32)] * 7,
        pltpu.VMEM((2 * HEADS, ROWS, ROWS), F32),
        pltpu.VMEM((HEADS, ROWS, 2 * BW), BF16),
        pltpu.VMEM((ROWS, BW), F32),
        pltpu.VMEM((6, ROWS, ROWS), F32),
        pltpu.VMEM((ROWS, BW), F32),
        pltpu.VMEM((1, WIDTH), F32),
        pltpu.VMEM((HEADS, 4, 8, BW), F32),
        pltpu.VMEM((SEQ_DEVICES, ROWS, ZY), F32),
        pltpu.VMEM((RING_Z, ROWS, YZ), F32),
        pltpu.VMEM((8, ROWS, ROWS), F32),
        pltpu.VMEM((8, ROWS, ROWS), F32),
        pltpu.VMEM((RING_Y, ROWS, WIDTH // RING_Y), BF16),
        pltpu.VMEM((RING_Z // 2, RING_Y, ROWS, YZ), BF16),
    ]
    scratch += [pltpu.VMEM((SEQ_DEVICES, 8, ROWS), F32) for _ in range(6)]
    for shape in (
        (Z_COUNT, RING_Y, PIECE, ZY),
        (Z_COUNT, PIECE, YZ),
        (RING_Y, ROWS, ZY),
    ):
        scratch += [pltpu.VMEM(shape, BF16), pltpu.VMEM(shape, BF16)]
    scratch += [
        pltpu.SemaphoreType.DMA((GROUPS, 4)),
        pltpu.SemaphoreType.DMA((6,)),
    ]
    quads = (RING_Z // 2, RING_Y)
    for shape in ((Z_COUNT,), (Z_COUNT,), (RING_Y,), quads, quads):
        scratch += [pltpu.SemaphoreType.DMA(shape), pltpu.SemaphoreType.DMA(shape)]
    scratch.append(pltpu.SemaphoreType.DMA((4,)))
    results = pl.pallas_call(
        kernel,
        out_shape=(
            pltpu.VMEM((ROWS, WIDTH), BF16),
            pltpu.VMEM((ROWS, WIDTH), BF16),
            pltpu.VMEM((ROWS, BW), F32),
            pltpu.VMEM((ROWS, BW), F32),
            pltpu.VMEM((8, ROWS), F32),
        ),
        in_specs=[smem, any_spec, any_spec, any_spec, vmem, vmem, vmem, any_spec],
        out_specs=(vmem,) * 5,
        scratch_shapes=scratch,
        compiler_params=pltpu.CompilerParams(
            collective_id=0, has_side_effects=True, vmem_limit_bytes=60 * 1024 * 1024
        ),
    )(
        docs,
        act,
        wi,
        wd,
        bi.reshape(1, WIDTH),
        bd.reshape(1, WIDTH),
        logits.reshape(1, WIDTH),
        cot,
    )
    results = [pltpu.with_memory_space_constraint(r, pltpu.VMEM) for r in results]
    outs = pl.pallas_call(
        hand_over,
        out_shape=[jax.ShapeDtypeStruct(a.shape, a.dtype) for a in results[:4]]
        + [jax.ShapeDtypeStruct((1, ROWS), F32)] * 3,
        in_specs=[vmem] * 5,
        out_specs=[any_spec] * 7,
        scratch_shapes=[pltpu.SemaphoreType.DMA((7,))],
    )(*results)
    return (*outs[:4], *(v.reshape(ROWS) for v in outs[4:]))


def solution(mesh):
    rows = P(("grp", "seq"), None)
    flat = P(("grp", "seq"))
    return jax.shard_map(
        on_device,
        mesh=mesh,
        in_specs=(rows, P(), P(), P(), P(), P(), P("grp"), rows),
        out_specs=(rows, rows, rows, rows, flat, flat, flat),
        check_vma=False,
    )
```
